128 devices in a mesh: ta: 16 (over y_hi, x, core), ha: 8 (over z, y_lo).
Axes of the slice: x: 4, y: 4 (y_hi: 2, y_lo: 2; y = y_hi * 2 + y_lo), z: 4, core: 2. Of those that a mesh axis runs over, the one named last changes fastest.
Arguments:
- query_seq: bfloat16 [32768, 1536], P(('ta', 'ha')), may hold values from -6 to 6
- key_seq: bfloat16 [32768, 1536], P(('ta', 'ha')), may hold values from -6 to 6
- value_seq: bfloat16 [32768, 1536], P(('ta', 'ha')), may hold values from -6 to 6
- tile_order: int32 [32768], replicated, may hold values from 0 to 32767, as said below
- grad_output: bfloat16 [64, 64, 8, 1536], P('ta', 'ha'), may hold values from -6 to 6
Outputs:
- attended: bfloat16 [64, 64, 8, 1536], P('ta', 'ha')
- grad_query: bfloat16 [64, 64, 8, 1536], P('ta', 'ha')
- grad_key: bfloat16 [64, 64, 8, 1536], P('ta', 'ha')
- grad_value: bfloat16 [64, 64, 8, 1536], P('ta', 'ha')
The draws below stay inside these ranges and needn't reach their ends.
Inputs may be any that keep to these rules, and one draw needn't show every extreme that they name: `tile_order`: A permutation of the raster indices; every aligned run of 256 sequence positions holds exactly 2 tokens of each aligned block of 4 frames by 8 rows.
All inputs are finite; a program needn't handle non-finite values.
Results may differ from the reference program's by a relative error of at most 0.0082.
Values may be sent and summed in bfloat16 or wider, within the bound.
A program may use at most 192 MiB of HBM per device.

```python
import jax
import jax.numpy as jnp
from jax import lax

HEADS = 12
HEAD_DIM = 128
TILE_FRAMES = 4
TILE_ROWS = 8
TILE_COLS = 8
BLOCK_FRAMES = 4
BLOCK_ROWS = 8
COLS = 8
CHANNELS = 1536
TOK_DEV = 256
FRAMES = 64
ROWS = 64
TOKENS = 32768
N_TA = 16
N_HA = 8


def raster_order(key):
    shard_count = N_TA * N_HA
    per_block = TOK_DEV // shard_count
    slot_keys = jax.random.split(jax.random.fold_in(key, 101), shard_count)
    seat_keys = jax.random.split(jax.random.fold_in(key, 202), shard_count)
    shuffle = jax.vmap(lambda one_key: jax.random.permutation(one_key, TOK_DEV))
    slot_perm = shuffle(slot_keys).astype(jnp.int32)
    seat_perm = shuffle(seat_keys).astype(jnp.int32)
    source = jnp.arange(shard_count, dtype=jnp.int32)[:, None]
    within = jnp.arange(TOK_DEV, dtype=jnp.int32)[None, :]
    target = within // per_block
    placed = seat_perm[target, source * per_block + within % per_block]
    frame_at = target // N_HA * BLOCK_FRAMES + placed // (BLOCK_ROWS * COLS)
    row_at = target % N_HA * BLOCK_ROWS + placed // COLS % BLOCK_ROWS
    column_at = placed % COLS
    raster = (frame_at * ROWS + row_at) * COLS + column_at
    inverse = jnp.argsort(slot_perm, axis=1)
    return jnp.take_along_axis(raster, inverse, axis=1).reshape(TOKENS).astype(jnp.int32)


def draw_tile_order(key, part):
    return raster_order(key)


def draw_query_seq(key, part):
    key = jax.random.fold_in(key, 1)
    return jnp.clip(jax.random.normal(key, (TOKENS, CHANNELS), jnp.float32), -6.0, 6.0).astype(jnp.bfloat16)


def draw_key_seq(key, part):
    key = jax.random.fold_in(key, 2)
    return jnp.clip(jax.random.normal(key, (TOKENS, CHANNELS), jnp.float32), -6.0, 6.0).astype(jnp.bfloat16)


def steps_of(own_key, shape, pieces, low, top_value):
    def one(position, shards_of):
        heights = jax.random.uniform(jax.random.fold_in(jax.random.fold_in(own_key, 6), position), (shards_of,), jnp.float32, low / len(pieces), top_value / len(pieces))
        return jnp.repeat(jnp.exp(heights), shape[position] // shards_of).reshape((-1,) + (1,) * (len(shape) - position - 1))

    factor_of = one(*pieces[0])
    for cut in pieces[1:]:
        factor_of = factor_of * one(*cut)
    return factor_of


def normal_values(key, extent, width, most, pieces=(), held_as=jnp.bfloat16):
    result = jax.random.normal(key, extent, jnp.float32) * width
    if len(pieces) > 0:
        result = steps_of(key, extent, pieces, -0.22, 0.18) * result
    return jnp.clip(result, min=-most, max=most).astype(held_as)


def setup_inputs(seed: int = 0) -> dict:
    splits = jax.random.split(jax.random.key(seed), 6)
    query_seq = draw_query_seq(jax.random.fold_in(splits[5], 71), 0)
    key_seq = draw_key_seq(jax.random.fold_in(splits[5], 71), 0)
    value_seq = normal_values(splits[2], (TOKENS, CHANNELS), 1.0, 6.0, ((0, 128),))
    tile_order = draw_tile_order(jax.random.fold_in(splits[5], 71), 0)
    grad_output = normal_values(splits[4], (FRAMES, ROWS, COLS, CHANNELS), 1.0, 6.0, ((0, 16), (1, 8)))
    return {"query_seq": query_seq, "key_seq": key_seq, "value_seq": value_seq, "tile_order": tile_order, "grad_output": grad_output}


score_floor = -1.0e30


def window_allowed(frame_first, row_first, total_frames, total_rows, block_frames, block_rows, grid_cols):
    query_frames = jnp.arange(block_frames) // TILE_FRAMES
    query_rows = jnp.arange(block_rows) // TILE_ROWS
    key_frames = jnp.arange(block_frames + 2 * TILE_FRAMES)
    key_rows = jnp.arange(block_rows + 2 * TILE_ROWS)
    frame_global = frame_first + key_frames - TILE_FRAMES
    row_global = row_first + key_rows - TILE_ROWS
    near_frames = jnp.abs(query_frames[:, None] - (key_frames[None, :] // TILE_FRAMES - 1)) <= 1
    near_frames = near_frames & ((frame_global >= 0) & (frame_global < total_frames))[None, :]
    near_rows = jnp.abs(query_rows[:, None] - (key_rows[None, :] // TILE_ROWS - 1)) <= 1
    near_rows = near_rows & ((row_global >= 0) & (row_global < total_rows))[None, :]
    col_tiles = jnp.arange(grid_cols) // TILE_COLS
    near_cols = jnp.abs(col_tiles[:, None] - col_tiles[None, :]) <= 1
    allowed = near_frames[:, None, None, :, None, None] & near_rows[None, :, None, None, :, None] & near_cols[None, None, :, None, None, :]
    ext_frames = block_frames + 2 * TILE_FRAMES
    ext_rows = block_rows + 2 * TILE_ROWS
    allowed = allowed.reshape(block_frames * block_rows * grid_cols, ext_frames * ext_rows * grid_cols)
    return allowed.astype(jnp.int32)


def head_pass(query_head, key_head, value_head, grad_head, allowed):
    score_scale = HEAD_DIM ** -0.5
    usable = allowed == 1
    scores = jnp.dot(query_head, key_head.T, preferred_element_type=jnp.float32) * score_scale
    scores = jnp.where(usable, scores, score_floor)
    row_top = jnp.max(scores, axis=1, keepdims=True)
    weights = jnp.where(usable, jnp.exp(scores - row_top), 0.0)
    row_total = jnp.sum(weights, axis=1, keepdims=True)
    probabilities = weights / row_total
    probs_low = probabilities.astype(jnp.bfloat16)
    out_full = jnp.dot(probs_low, value_head, preferred_element_type=jnp.float32)
    grad_prob = jnp.dot(grad_head, value_head.T, preferred_element_type=jnp.float32)
    row_delta = jnp.sum(grad_head.astype(jnp.float32) * out_full, axis=1, keepdims=True)
    grad_score = (probabilities * (grad_prob - row_delta) * score_scale).astype(jnp.bfloat16)
    grad_query = jnp.dot(grad_score, key_head, preferred_element_type=jnp.float32).astype(jnp.bfloat16)
    grad_key = jnp.dot(grad_score.T, query_head, preferred_element_type=jnp.float32)
    grad_value = jnp.dot(probs_low.T, grad_head, preferred_element_type=jnp.float32)
    return out_full.astype(jnp.bfloat16), grad_query, grad_key, grad_value


def split_heads(matrix):
    return matrix.reshape(matrix.shape[0], HEADS, HEAD_DIM).transpose(1, 0, 2)


def join_heads(stacked):
    return stacked.transpose(1, 0, 2).reshape(stacked.shape[1], HEADS * HEAD_DIM)


def all_heads(query_rows, key_ext, value_ext, grad_rows, allowed):
    def one_head(head_parts):
        return head_pass(head_parts[0], head_parts[1], head_parts[2], head_parts[3], allowed)

    results = lax.map(one_head, (split_heads(query_rows), split_heads(key_ext), split_heads(value_ext), split_heads(grad_rows)))
    return tuple(join_heads(member) for member in results)


def reference(query_seq, key_seq, value_seq, tile_order, grad_output):
    def to_grid(seq_rows):
        placed = jnp.zeros_like(seq_rows).at[tile_order].set(seq_rows)
        return placed.reshape(FRAMES, ROWS, COLS, CHANNELS)

    query_grid = to_grid(query_seq)
    key_grid = to_grid(key_seq)
    value_grid = to_grid(value_seq)
    pad_spec = ((TILE_FRAMES, TILE_FRAMES), (TILE_ROWS, TILE_ROWS), (0, 0), (0, 0))
    key_pad = jnp.pad(key_grid, pad_spec)
    value_pad = jnp.pad(value_grid, pad_spec)
    ext_frames = BLOCK_FRAMES + 2 * TILE_FRAMES
    ext_rows = BLOCK_ROWS + 2 * TILE_ROWS
    ext_shape = (ext_frames, ext_rows, COLS, CHANNELS)
    zero_index = jnp.zeros((), jnp.int32)
    empty_pad = jnp.zeros((FRAMES + 2 * TILE_FRAMES, ROWS + 2 * TILE_ROWS, COLS, CHANNELS), jnp.float32)
    frame_span = jnp.arange(ext_frames)
    row_span = jnp.arange(ext_rows)
    inside_frames = (frame_span >= TILE_FRAMES) & (frame_span < TILE_FRAMES + BLOCK_FRAMES)
    inside_rows = (row_span >= TILE_ROWS) & (row_span < TILE_ROWS + BLOCK_ROWS)
    inside = inside_frames[:, None, None, None] & inside_rows[None, :, None, None]

    def settle(grad_ext):
        shaped = grad_ext.reshape(ext_shape)
        rounded = lax.optimization_barrier(shaped.astype(jnp.bfloat16)).astype(jnp.float32)
        return jnp.where(inside, shaped, rounded)

    def block_step(carried, block_index):
        grad_key_pad, grad_value_pad = carried
        frame_first = ((block_index // N_HA) * BLOCK_FRAMES).astype(jnp.int32)
        row_first = ((block_index % N_HA) * BLOCK_ROWS).astype(jnp.int32)
        starts = (frame_first, row_first, zero_index, zero_index)
        query_block = lax.dynamic_slice(query_grid, starts, (BLOCK_FRAMES, BLOCK_ROWS, COLS, CHANNELS)).reshape(-1, CHANNELS)
        grad_block = lax.dynamic_slice(grad_output, starts, (BLOCK_FRAMES, BLOCK_ROWS, COLS, CHANNELS)).reshape(-1, CHANNELS)
        key_block = lax.dynamic_slice(key_pad, starts, ext_shape).reshape(-1, CHANNELS)
        value_block = lax.dynamic_slice(value_pad, starts, ext_shape).reshape(-1, CHANNELS)
        allowed = window_allowed(frame_first, row_first, FRAMES, ROWS, BLOCK_FRAMES, BLOCK_ROWS, COLS)
        attended, grad_query, grad_key_ext, grad_value_ext = all_heads(query_block, key_block, value_block, grad_block, allowed)
        previous = lax.dynamic_slice(grad_key_pad, starts, ext_shape)
        grad_key_pad = lax.dynamic_update_slice(grad_key_pad, previous + settle(grad_key_ext), starts)
        previous = lax.dynamic_slice(grad_value_pad, starts, ext_shape)
        grad_value_pad = lax.dynamic_update_slice(grad_value_pad, previous + settle(grad_value_ext), starts)
        return (grad_key_pad, grad_value_pad), (attended, grad_query)

    finals, blocks = lax.scan(block_step, (empty_pad, empty_pad), jnp.arange(N_TA * N_HA, dtype=jnp.int32))

    def to_tiles(stacked):
        shaped = stacked.reshape(N_TA, N_HA, BLOCK_FRAMES, BLOCK_ROWS, COLS, CHANNELS)
        return shaped.transpose(0, 2, 1, 3, 4, 5).reshape(FRAMES, ROWS, COLS, CHANNELS)

    grad_key = finals[0][TILE_FRAMES:TILE_FRAMES + FRAMES, TILE_ROWS:TILE_ROWS + ROWS].astype(jnp.bfloat16)
    grad_value = finals[1][TILE_FRAMES:TILE_FRAMES + FRAMES, TILE_ROWS:TILE_ROWS + ROWS].astype(jnp.bfloat16)
    return to_tiles(blocks[0]), to_tiles(blocks[1]), grad_key, grad_value
```

```python
import functools

import jax
import jax.numpy as jnp
from jax import lax
from jax.experimental import pallas as pl
from jax.experimental.pallas import tpu as pltpu
from jax.sharding import PartitionSpec as P

HEADS = 12
HEAD_DIM = 128
GROUP_HEADS = 3
TILE_FRAMES = 4
TILE_ROWS = 8
SCALE = HEAD_DIM ** (-0.5)
LOG2E = 1.4426950408889634
NEG = -1e30
MESH = pl.DeviceIdType.MESH
F32 = jnp.float32
BF16 = jnp.bfloat16
DIRECTIONS = [(a, b) for a in (-1, 0, 1) for b in (-1, 0, 1) if (a, b) != (0, 0)]


def dot(a, b):
    return jnp.dot(a, b, preferred_element_type=F32)


def dot_nt(a, b):
    return lax.dot_general(a, b, (((1,), (1,)), ((), ())), preferred_element_type=F32)


def iota(shape, dim):
    return lax.broadcasted_iota(jnp.int32, shape, dim)


def own_part(step):
    return {1: 2, -1: 1, 0: pl.ds(1, 2)}[step]


def halo_part(step):
    return {1: 3, -1: 0, 0: pl.ds(1, 2)}[step]


def kernel(
    nt, nh, cols,
    q_ref, k_ref, v_ref, order_ref, grad_ref,
    att_ref, dq_ref, dk_ref, dv_ref,
    pair, sort_one, send, recv, place, ext, ext_t, query_t, grad_blocks, grad_t,
    score, prob, acc, own_acc, back_send, back_recv, stage,
    pair_sem, pair_send_sem, pair_recv_sem,
    grad_sem, grad_send_sem, grad_recv_sem,
    all_sem, all_send_sem, all_recv_sem,
    halo_send_sem, halo_recv_sem, back_send_sem, back_recv_sem,
    out_sem, out_send_sem, out_recv_sem,
):
    tok = TILE_FRAMES * TILE_ROWS * cols
    nk, nz = nt // 2, nh // 2
    chips = nk * nh
    width = GROUP_HEADS * HEAD_DIM
    ta, ha = lax.axis_index("ta"), lax.axis_index("ha")
    kk, core = ta // 2, ta % 2
    zz, half = ha // 2, ha % 2
    chip = kk * nh + ha
    others = [(1 - core, half), (core, 1 - half), (1 - core, 1 - half)]

    def mate(where):
        return (2 * kk + where[0], 2 * zz + where[1])

    def exists(dk, dz):
        okay = []
        if dk < 0:
            okay.append(kk > 0)
        if dk > 0:
            okay.append(kk < nk - 1)
        if dz < 0:
            okay.append(zz > 0)
        if dz > 0:
            okay.append(zz < nz - 1)
        return functools.reduce(jnp.logical_and, okay)

    for there, index in (
        (kk == 0, (0, slice(None))),
        (kk == nk - 1, (3, slice(None))),
        (zz == 0, (slice(None), 0)),
        (zz == nz - 1, (slice(None), 3)),
    ):

        @pl.when(there)
        def _():
            def clear(h, carry):
                for n in range(4):
                    at = tuple(n if isinstance(x, slice) else x for x in index)
                    ext[(h,) + at] = jnp.zeros((tok, 2 * HEAD_DIM), BF16)
                    back_recv[(h,) + at] = jnp.zeros((tok, 2 * HEAD_DIM), BF16)
                return carry

            lax.fori_loop(0, GROUP_HEADS, clear, 0)

    barrier = pltpu.get_barrier_semaphore()

    def greet(d, carry):
        to = lax.rem(chip + d, chips)
        pl.semaphore_signal(
            barrier, inc=1, device_id=(2 * (to // nh) + core, to % nh), device_id_type=MESH
        )
        return carry

    lax.fori_loop(1, chips, greet, 0)
    for where in ((1 - core, half), (1 - core, 1 - half)):
        pl.semaphore_signal(barrier, inc=1, device_id=mate(where), device_id_type=MESH)

    seq = (q_ref, k_ref, v_ref)
    pair_width = 2 * width
    own_cols = pl.ds(pl.multiple_of(core * pair_width, pair_width), pair_width)
    far_cols = pl.ds(pl.multiple_of((1 - core) * pair_width, pair_width), pair_width)
    own_rows = pl.ds(pl.multiple_of(core * tok, tok), tok)
    for a in range(3):
        pltpu.make_async_copy(
            seq[a].at[:, own_cols], pair.at[a, own_rows], pair_sem.at[a]
        ).start()

    def group_cols(where, n=width):
        return pl.ds(pl.multiple_of((2 * where[0] + where[1]) * width, width), width)

    own_block = 2 * core + half
    pltpu.make_async_copy(
        grad_ref.at[:, group_cols((core, half))], grad_blocks.at[own_block], grad_sem
    ).start()

    pl.semaphore_wait(barrier, chips + 1)

    def pair_copy(a):
        return pltpu.make_async_remote_copy(
            src_ref=seq[a].at[:, far_cols],
            dst_ref=pair.at[a, own_rows],
            send_sem=pair_send_sem.at[a],
            recv_sem=pair_recv_sem.at[a],
            device_id=mate((1 - core, half)),
            device_id_type=MESH,
        )

    def grad_copy(n):
        return pltpu.make_async_remote_copy(
            src_ref=grad_ref.at[:, group_cols(others[n])],
            dst_ref=grad_blocks.at[own_block],
            send_sem=grad_send_sem.at[n],
            recv_sem=grad_recv_sem.at[n],
            device_id=mate(others[n]),
            device_id_type=MESH,
        )

    for a in range(3):
        pair_copy(a).start()
    for n in range(3):
        grad_copy(n).start()

    def decode(t):
        frame = t // (nh * TILE_ROWS * cols)
        row = (t // cols) % (nh * TILE_ROWS)
        frame_block, row_block = frame // TILE_FRAMES, row // TILE_ROWS
        inside = ((frame % TILE_FRAMES) * TILE_ROWS + row % TILE_ROWS) * cols + t % cols
        return frame_block, row_block, inside

    order = order_ref[...]
    order_t = order.T
    for cc in range(2):
        source = kk * 2 * nh + cc * nh + ha
        line = order_ref[pl.ds(source, 1), :]
        column = jnp.sum(
            jnp.where(iota(order_t.shape, 1) == source, order_t, 0), axis=1, keepdims=True
        )
        line_f, line_r, _ = decode(line)
        col_f, col_r, _ = decode(column)
        same = (line_f * nh + line_r) == (col_f * nh + col_r)
        earlier = iota((tok, tok), 0) < iota((tok, tok), 1)
        second = jnp.sum(jnp.where(same & earlier, 1, 0), axis=0, keepdims=True)
        region = (line_f // 2) * nz + line_r // 2
        seat = region * 16 + ((line_f % 2) * 2 + line_r % 2) * 4 + cc * 2 + second
        sort_one[:, cc * tok : (cc + 1) * tok] = jnp.where(
            iota((2 * tok, tok), 0) == seat, 1.0, 0.0
        ).astype(BF16)

    for a in range(3):
        pltpu.make_async_copy(
            seq[a].at[:, own_cols], pair.at[a, own_rows], pair_sem.at[a]
        ).wait()
        pair_copy(a).wait_recv()

    def all_copy(h, d):
        to = lax.rem(chip + d, chips)
        to_k, to_h = to // nh, to % nh
        region = to_k * nz + to_h // 2
        return pltpu.make_async_remote_copy(
            src_ref=send.at[h, to_h % 2, pl.ds(pl.multiple_of(region * 16, 16), 16)],
            dst_ref=recv.at[h, pl.ds(pl.multiple_of(chip * 16, 16), 16)],
            send_sem=all_send_sem.at[h],
            recv_sem=all_recv_sem.at[h],
            device_id=(2 * to_k + core, to_h),
            device_id_type=MESH,
        )

    def all_own(h):
        region = kk * nz + zz
        return pltpu.make_async_copy(
            send.at[h, half, pl.ds(pl.multiple_of(region * 16, 16), 16)],
            recv.at[h, pl.ds(pl.multiple_of(chip * 16, 16), 16)],
            all_sem.at[h],
        )

    def send_head(h, carry):
        for a in range(3):
            left = pl.ds(pl.multiple_of(h * HEAD_DIM, HEAD_DIM), HEAD_DIM)
            right = pl.ds(pl.multiple_of(width + h * HEAD_DIM, HEAD_DIM), HEAD_DIM)
            both = jnp.concatenate([pair[a, :, left], pair[a, :, right]], axis=1)
            sorted_rows = dot(sort_one[...], both).astype(BF16)
            into = slice(a * HEAD_DIM, (a + 1) * HEAD_DIM)
            send[h, 0, :, into] = sorted_rows[:, :HEAD_DIM]
            send[h, 1, :, into] = sorted_rows[:, HEAD_DIM:]
        all_own(h).start()

        def push(d, inner):
            all_copy(h, d).start()
            return inner

        lax.fori_loop(1, chips, push, 0)
        return carry

    lax.fori_loop(0, GROUP_HEADS, send_head, 0)

    frame_block, row_block, inside = decode(order_t)
    block_of = frame_block * nh + row_block
    code = iota(order_t.shape, 0) * tok + inside
    found = []
    for b in range(4):
        mine = block_of == (2 * kk + b // 2) * nh + 2 * zz + b % 2
        found.append(jnp.min(jnp.where(mine, code, tok * tok), axis=0, keepdims=True) % tok)
        found.append(jnp.max(jnp.where(mine, code, 0), axis=0, keepdims=True) % tok)
    table = jnp.concatenate(found, axis=0).astype(F32).astype(BF16)
    rows = 4 * tok
    number = iota((nt * nh, rows), 1)
    from_chip, place_in = number // 16, number % 16
    sender = (from_chip // nh) * 2 * nh + ((place_in // 2) % 2) * nh + from_chip % nh
    spread = jnp.where(iota((nt * nh, rows), 0) == sender, 1.0, 0.0).astype(BF16)
    wide = dot(table, spread)
    lane = iota((8, rows), 1) % 16
    chosen = iota((8, rows), 0) == (lane // 4) * 2 + lane % 2
    position = jnp.sum(jnp.where(chosen, wide, 0.0), axis=0, keepdims=True).astype(jnp.int32)
    position = position + (iota((1, rows), 1) % 16 // 4) * tok

    def fill_place(b, carry):
        place[b] = jnp.where(iota((tok, rows), 0) + b * tok == position, 1.0, 0.0).astype(BF16)
        return carry

    lax.fori_loop(0, 4, fill_place, 0)

    pltpu.make_async_copy(
        grad_ref.at[:, group_cols((core, half))], grad_blocks.at[own_block], grad_sem
    ).wait()
    for n in range(3):
        grad_copy(n).wait_recv()

    def turn_grad(b, carry):
        for h in range(GROUP_HEADS):
            piece = grad_blocks[b, :, h * HEAD_DIM : (h + 1) * HEAD_DIM]
            grad_t[h, b] = piece.astype(F32).T.astype(BF16)
        return carry

    lax.fori_loop(0, 4, turn_grad, 0)

    def halo_copy(h, n):
        dk, dz = DIRECTIONS[n]
        return pltpu.make_async_remote_copy(
            src_ref=ext.at[h, own_part(dk), own_part(dz)],
            dst_ref=ext.at[h, halo_part(-dk), halo_part(-dz)],
            send_sem=halo_send_sem.at[h, n],
            recv_sem=halo_recv_sem.at[h, n],
            device_id=(ta + 2 * dk, ha + 2 * dz),
            device_id_type=MESH,
        )

    def back_copy(h, n):
        dk, dz = DIRECTIONS[n]
        return pltpu.make_async_remote_copy(
            src_ref=back_send.at[h, halo_part(dk), halo_part(dz)],
            dst_ref=back_recv.at[h, halo_part(-dk), halo_part(-dz)],
            send_sem=back_send_sem.at[h, n],
            recv_sem=back_recv_sem.at[h, n],
            device_id=(ta + 2 * dk, ha + 2 * dz),
            device_id_type=MESH,
        )

    def each_sent(step):
        for n, (dk, dz) in enumerate(DIRECTIONS):
            pl.when(exists(dk, dz))(functools.partial(step, n))

    def each_arrival(step):
        for n, (dk, dz) in enumerate(DIRECTIONS):
            pl.when(exists(-dk, -dz))(functools.partial(step, n))

    def settle(h, carry):
        all_own(h).wait()
        many = pl.ds(0, 16 * (chips - 1))
        pltpu.make_async_copy(recv.at[h, many], recv.at[h, many], all_recv_sem.at[h]).wait()

        def one_block(b, inner):
            grid_rows = dot(place[b], recv[h])
            query_t[h, b] = grid_rows[:, :HEAD_DIM].T.astype(BF16)
            ext[h, 1 + b // 2, 1 + b % 2] = grid_rows[:, HEAD_DIM:].astype(BF16)
            return inner

        lax.fori_loop(0, 4, one_block, 0)
        each_sent(lambda n: halo_copy(h, n).start())
        return carry

    lax.fori_loop(0, GROUP_HEADS, settle, 0)

    outs = (att_ref, dq_ref, dk_ref, dv_ref)

    def out_cols(h):
        first = ((2 * core + half) * GROUP_HEADS + h) * HEAD_DIM
        return pl.ds(pl.multiple_of(first, HEAD_DIM), HEAD_DIM)

    def out_copy(o, h, n):
        return pltpu.make_async_remote_copy(
            src_ref=stage.at[o, h, 2 * others[n][0] + others[n][1]],
            dst_ref=outs[o].at[:, out_cols(h)],
            send_sem=out_send_sem.at[o],
            recv_sem=out_recv_sem.at[o],
            device_id=mate(others[n]),
            device_id_type=MESH,
        )

    def out_own(o, h):
        return pltpu.make_async_copy(
            stage.at[o, h, own_block], outs[o].at[:, out_cols(h)], out_sem.at[o]
        )

    def hand_out(o, h):
        for n in range(3):
            out_copy(o, h, n).start()
        out_own(o, h).start()

    def attend(h, carry):
        each_arrival(lambda n: halo_copy(h, n).wait_recv())

        def prepare(e, inner):
            ext_t[e // 4, e % 4] = ext[h, e // 4, e % 4].astype(F32).T.astype(BF16)
            acc[e // 4, e % 4] = jnp.zeros((tok, 2 * HEAD_DIM), F32)
            return inner

        lax.fori_loop(0, 16, prepare, 0)

        def one_block(b, inner):
            bi, bj = b // 2, b % 2
            q_t, g_t = query_t[h, b], grad_t[h, b]
            spots = [(bi + di, bj + dj) for di in range(3) for dj in range(3)]
            biases = []
            for i, j in spots:
                missing = (
                    ((kk == 0) & (i == 0))
                    | ((kk == nk - 1) & (i == 3))
                    | ((zz == 0) & (j == 0))
                    | ((zz == nz - 1) & (j == 3))
                )
                biases.append(jnp.where(missing, NEG, 0.0).astype(F32))
            top = jnp.full((1, tok), NEG, F32)
            for n, (i, j) in enumerate(spots):
                s = dot(ext[h, i, j, :, :HEAD_DIM], q_t)
                score[n] = s
                top = jnp.maximum(top, jnp.max(s, axis=0, keepdims=True) + biases[n])
            shift = top * (SCALE * LOG2E)
            total = jnp.zeros((1, tok), F32)
            out_t = jnp.zeros((HEAD_DIM, tok), F32)
            for n, (i, j) in enumerate(spots):
                p = jnp.exp2(score[n] * (SCALE * LOG2E) - (shift - biases[n]))
                total = total + jnp.sum(p, axis=0, keepdims=True)
                p_low = p.astype(BF16)
                prob[n] = p_low
                out_t = out_t + dot(ext_t[i, j, HEAD_DIM:, :], p_low)
            inverse = 1.0 / total
            out_t = out_t * inverse
            grad_f = g_t.astype(F32)
            delta = jnp.sum(grad_f * out_t, axis=0, keepdims=True)
            stage[0, h, b] = out_t.T.astype(BF16)
            g_scaled = (grad_f * inverse).astype(BF16)
            q_scaled = (q_t.astype(F32) * (inverse * SCALE)).astype(BF16)
            dq_t = jnp.zeros((HEAD_DIM, tok), F32)
            for n, (i, j) in enumerate(spots):
                dp = dot(ext[h, i, j, :, HEAD_DIM:], g_t)
                p_low = prob[n]
                ds = (p_low.astype(F32) * (dp - delta)).astype(BF16)
                dq_t = dq_t + dot(ext_t[i, j, :HEAD_DIM, :], ds)
                acc[i, j, :, :HEAD_DIM] += dot_nt(ds, q_scaled)
                acc[i, j, :, HEAD_DIM:] += dot_nt(p_low, g_scaled)
            stage[1, h, b] = (dq_t * (inverse * SCALE)).T.astype(BF16)
            return inner

        lax.fori_loop(0, 4, one_block, 0)

        def put_back(e, inner):
            back_send[h, e // 4, e % 4] = acc[e // 4, e % 4].astype(BF16)
            return inner

        lax.fori_loop(0, 16, put_back, 0)
        each_sent(lambda n: back_copy(h, n).start())
        hand_out(0, h)
        hand_out(1, h)

        def keep(b, inner):
            own_acc[h, b] = acc[1 + b // 2, 1 + b % 2]
            return inner

        lax.fori_loop(0, 4, keep, 0)
        return carry

    lax.fori_loop(0, GROUP_HEADS, attend, 0)

    def finish(h, carry):
        each_arrival(lambda n: back_copy(h, n).wait_recv())

        def one_block(b, inner):
            bi, bj = b // 2, b % 2
            far_i, far_j = 3 * bi, 3 * bj
            total = own_acc[h, b]
            for i, j in ((far_i, 1 + bj), (1 + bi, far_j), (far_i, far_j)):
                total = total + back_recv[h, i, j].astype(F32)
            low = total.astype(BF16)
            stage[2, h, b] = low[:, :HEAD_DIM]
            stage[3, h, b] = low[:, HEAD_DIM:]
            return inner

        lax.fori_loop(0, 4, one_block, 0)
        hand_out(2, h)
        hand_out(3, h)
        return carry

    lax.fori_loop(0, GROUP_HEADS, finish, 0)

    for a in range(3):
        pair_copy(a).wait_send()
    for n in range(3):
        grad_copy(n).wait_send()

    def sent(h, carry):
        many = pl.ds(0, 16 * (chips - 1))
        pltpu.make_async_copy(recv.at[h, many], recv.at[h, many], all_send_sem.at[h]).wait()
        each_sent(lambda n: halo_copy(h, n).wait_send())
        each_sent(lambda n: back_copy(h, n).wait_send())
        return carry

    lax.fori_loop(0, GROUP_HEADS, sent, 0)
    for o in range(4):
        mine = outs[o].at[:, pl.ds(0, width)]
        far = outs[o].at[:, pl.ds(0, 3 * width)]
        pltpu.make_async_copy(mine, mine, out_sem.at[o]).wait()
        pltpu.make_async_copy(far, far, out_send_sem.at[o]).wait()
        pltpu.make_async_copy(far, far, out_recv_sem.at[o]).wait()


def shards(nt, nh, query_seq, key_seq, value_seq, tile_order, grad_output):
    block_shape = grad_output.shape
    cols = block_shape[2]
    tok, channels = query_seq.shape
    low = jax.ShapeDtypeStruct((tok, channels), BF16)
    hbm = pl.BlockSpec(memory_space=pl.ANY)
    vmem = pl.BlockSpec(memory_space=pltpu.VMEM)
    gh, d = GROUP_HEADS, HEAD_DIM
    dma = pltpu.SemaphoreType.DMA
    outs = pl.pallas_call(
        functools.partial(kernel, nt, nh, cols),
        out_shape=[low] * 4,
        in_specs=[hbm, hbm, hbm, vmem, hbm],
        out_specs=[hbm] * 4,
        scratch_shapes=[
            pltpu.VMEM((3, 2 * tok, 2 * gh * d), BF16),
            pltpu.VMEM((2 * tok, 2 * tok), BF16),
            pltpu.VMEM((gh, 2, 2 * tok, 3 * d), BF16),
            pltpu.VMEM((gh, 4 * tok, 3 * d), BF16),
            pltpu.VMEM((4, tok, 4 * tok), BF16),
            pltpu.VMEM((gh, 4, 4, tok, 2 * d), BF16),
            pltpu.VMEM((4, 4, 2 * d, tok), BF16),
            pltpu.VMEM((gh, 4, d, tok), BF16),
            pltpu.VMEM((4, tok, gh * d), BF16),
            pltpu.VMEM((gh, 4, d, tok), BF16),
            pltpu.VMEM((9, tok, tok), F32),
            pltpu.VMEM((9, tok, tok), BF16),
            pltpu.VMEM((4, 4, tok, 2 * d), F32),
            pltpu.VMEM((gh, 4, tok, 2 * d), F32),
            pltpu.VMEM((gh, 4, 4, tok, 2 * d), BF16),
            pltpu.VMEM((gh, 4, 4, tok, 2 * d), BF16),
            pltpu.VMEM((4, gh, 4, tok, d), BF16),
            dma((3,)), dma((3,)), dma((3,)),
            dma, dma((3,)), dma((3,)),
            dma((gh,)), dma((gh,)), dma((gh,)),
            dma((gh, 8)), dma((gh, 8)), dma((gh, 8)), dma((gh, 8)),
            dma((4,)), dma((4,)), dma((4,)),
        ],
        compiler_params=pltpu.CompilerParams(
            collective_id=0, has_side_effects=True, vmem_limit_bytes=60 * 2**20
        ),
        cost_estimate=pl.CostEstimate(
            flops=12 * 4 * gh * 9 * tok * tok * d,
            bytes_accessed=16 * tok * channels,
            transcendentals=4 * gh * 9 * tok * tok,
        ),
    )(query_seq, key_seq, value_seq, tile_order.reshape(nt * nh, tok), grad_output.reshape(tok, channels))
    return tuple(o.reshape(block_shape) for o in outs)


def solution(mesh):
    seq = P(("ta", "ha"), None)
    grid = P("ta", "ha", None, None)
    return jax.shard_map(
        functools.partial(shards, mesh.shape["ta"], mesh.shape["ha"]),
        mesh=mesh,
        in_specs=(seq, seq, seq, P(), grid),
        out_specs=(grid,) * 4,
        check_vma=False,
    )
```

```python
import functools

import jax
import jax.numpy as jnp
from jax import lax
from jax.experimental import pallas as pl
from jax.experimental.pallas import tpu as pltpu
from jax.sharding import PartitionSpec as P

HEADS = 12
HEAD_DIM = 128
GROUP_HEADS = 3
TILE_FRAMES = 4
TILE_ROWS = 8
SCALE = HEAD_DIM ** (-0.5)
LOG2E = 1.4426950408889634
NEG = -1e30
MESH = pl.DeviceIdType.MESH
F32 = jnp.float32
BF16 = jnp.bfloat16
DIRECTIONS = [(a, b) for a in (-1, 0, 1) for b in (-1, 0, 1) if (a, b) != (0, 0)]


def dot(a, b):
    return jnp.dot(a, b, preferred_element_type=F32)


def dot_nt(a, b):
    return lax.dot_general(a, b, (((1,), (1,)), ((), ())), preferred_element_type=F32)


def iota(shape, dim):
    return lax.broadcasted_iota(jnp.int32, shape, dim)


def own_part(step):
    return {1: 2, -1: 1, 0: pl.ds(1, 2)}[step]


def halo_part(step):
    return {1: 3, -1: 0, 0: pl.ds(1, 2)}[step]


def kernel(
    nt, nh, cols,
    q_ref, k_ref, v_ref, order_ref, grad_ref,
    att_ref, dq_ref, dk_ref, dv_ref,
    pair, sort_one, send, recv, place, ext, ext_t, query_t, grad_blocks, grad_t,
    score, prob, acc, own_acc, back_send, back_recv, stage,
    pair_sem, pair_send_sem, pair_recv_sem,
    grad_sem, grad_send_sem, grad_recv_sem,
    all_sem, all_send_sem, all_recv_sem,
    halo_send_sem, halo_recv_sem, back_send_sem, back_recv_sem,
    out_sem, out_send_sem, out_recv_sem,
):
    tok = TILE_FRAMES * TILE_ROWS * cols
    nk, nz = nt // 2, nh // 2
    chips = nk * nh
    width = GROUP_HEADS * HEAD_DIM
    ta, ha = lax.axis_index("ta"), lax.axis_index("ha")
    kk, core = ta // 2, ta % 2
    zz, half = ha // 2, ha % 2
    chip = kk * nh + ha
    others = [(1 - core, half), (core, 1 - half), (1 - core, 1 - half)]

    def mate(where):
        return (2 * kk + where[0], 2 * zz + where[1])

    def exists(dk, dz):
        okay = []
        if dk < 0:
            okay.append(kk > 0)
        if dk > 0:
            okay.append(kk < nk - 1)
        if dz < 0:
            okay.append(zz > 0)
        if dz > 0:
            okay.append(zz < nz - 1)
        return functools.reduce(jnp.logical_and, okay)

    for there, index in (
        (kk == 0, (0, slice(None))),
        (kk == nk - 1, (3, slice(None))),
        (zz == 0, (slice(None), 0)),
        (zz == nz - 1, (slice(None), 3)),
    ):

        @pl.when(there)
        def _():
            def clear(h, carry):
                for n in range(4):
                    at = tuple(n if isinstance(x, slice) else x for x in index)
                    ext[(h,) + at] = jnp.zeros((tok, 2 * HEAD_DIM), BF16)
                    back_recv[(h,) + at] = jnp.zeros((tok, 2 * HEAD_DIM), BF16)
                return carry

            lax.fori_loop(0, GROUP_HEADS, clear, 0)

    barrier = pltpu.get_barrier_semaphore()

    def greet(d, carry):
        to = lax.rem(chip + d, chips)
        pl.semaphore_signal(
            barrier, inc=1, device_id=(2 * (to // nh) + core, to % nh), device_id_type=MESH
        )
        return carry

    lax.fori_loop(1, chips, greet, 0)
    for where in ((1 - core, half), (1 - core, 1 - half)):
        pl.semaphore_signal(barrier, inc=1, device_id=mate(where), device_id_type=MESH)

    seq = (q_ref, k_ref, v_ref)
    pair_width = 2 * width
    own_cols = pl.ds(pl.multiple_of(core * pair_width, pair_width), pair_width)
    far_cols = pl.ds(pl.multiple_of((1 - core) * pair_width, pair_width), pair_width)
    own_rows = pl.ds(pl.multiple_of(core * tok, tok), tok)
    for a in range(3):
        pltpu.make_async_copy(
            seq[a].at[:, own_cols], pair.at[a, own_rows], pair_sem.at[a]
        ).start()

    def group_cols(where, n=width):
        return pl.ds(pl.multiple_of((2 * where[0] + where[1]) * width, width), width)

    own_block = 2 * core + half
    pltpu.make_async_copy(
        grad_ref.at[:, group_cols((core, half))], grad_blocks.at[own_block], grad_sem
    ).start()

    pl.semaphore_wait(barrier, chips + 1)

    def pair_copy(a):
        return pltpu.make_async_remote_copy(
            src_ref=seq[a].at[:, far_cols],
            dst_ref=pair.at[a, own_rows],
            send_sem=pair_send_sem.at[a],
            recv_sem=pair_recv_sem.at[a],
            device_id=mate((1 - core, half)),
            device_id_type=MESH,
        )

    def grad_copy(n):
        return pltpu.make_async_remote_copy(
            src_ref=grad_ref.at[:, group_cols(others[n])],
            dst_ref=grad_blocks.at[own_block],
            send_sem=grad_send_sem.at[n],
            recv_sem=grad_recv_sem.at[n],
            device_id=mate(others[n]),
            device_id_type=MESH,
        )

    for a in range(3):
        pair_copy(a).start()
    for n in range(3):
        grad_copy(n).start()

    def decode(t):
        frame = t // (nh * TILE_ROWS * cols)
        row = (t // cols) % (nh * TILE_ROWS)
        frame_block, row_block = frame // TILE_FRAMES, row // TILE_ROWS
        inside = ((frame % TILE_FRAMES) * TILE_ROWS + row % TILE_ROWS) * cols + t % cols
        return frame_block, row_block, inside

    order = order_ref[...]
    order_t = order.T
    for cc in range(2):
        source = kk * 2 * nh + cc * nh + ha
        line = order_ref[pl.ds(source, 1), :]
        column = jnp.sum(
            jnp.where(iota(order_t.shape, 1) == source, order_t, 0), axis=1, keepdims=True
        )
        line_f, line_r, _ = decode(line)
        col_f, col_r, _ = decode(column)
        same = (line_f * nh + line_r) == (col_f * nh + col_r)
        earlier = iota((tok, tok), 0) < iota((tok, tok), 1)
        second = jnp.sum(jnp.where(same & earlier, 1, 0), axis=0, keepdims=True)
        region = (line_f // 2) * nz + line_r // 2
        seat = region * 16 + ((line_f % 2) * 2 + line_r % 2) * 4 + cc * 2 + second
        sort_one[:, cc * tok : (cc + 1) * tok] = jnp.where(
            iota((2 * tok, tok), 0) == seat, 1.0, 0.0
        ).astype(BF16)

    for a in range(3):
        pltpu.make_async_copy(
            seq[a].at[:, own_cols], pair.at[a, own_rows], pair_sem.at[a]
        ).wait()
        pair_copy(a).wait_recv()

    def all_copy(h, d):
        to = lax.rem(chip + d, chips)
        to_k, to_h = to // nh, to % nh
        region = to_k * nz + to_h // 2
        return pltpu.make_async_remote_copy(
            src_ref=send.at[h, to_h % 2, pl.ds(pl.multiple_of(region * 16, 16), 16)],
            dst_ref=recv.at[h, pl.ds(pl.multiple_of(chip * 16, 16), 16)],
            send_sem=all_send_sem.at[h],
            recv_sem=all_recv_sem.at[h],
            device_id=(2 * to_k + core, to_h),
            device_id_type=MESH,
        )

    def all_own(h):
        region = kk * nz + zz
        return pltpu.make_async_copy(
            send.at[h, half, pl.ds(pl.multiple_of(region * 16, 16), 16)],
            recv.at[h, pl.ds(pl.multiple_of(chip * 16, 16), 16)],
            all_sem.at[h],
        )

    def send_head(h, carry):
        for a in range(3):
            left = pl.ds(pl.multiple_of(h * HEAD_DIM, HEAD_DIM), HEAD_DIM)
            right = pl.ds(pl.multiple_of(width + h * HEAD_DIM, HEAD_DIM), HEAD_DIM)
            both = jnp.concatenate([pair[a, :, left], pair[a, :, right]], axis=1)
            sorted_rows = dot(sort_one[...], both).astype(BF16)
            into = slice(a * HEAD_DIM, (a + 1) * HEAD_DIM)
            send[h, 0, :, into] = sorted_rows[:, :HEAD_DIM]
            send[h, 1, :, into] = sorted_rows[:, HEAD_DIM:]
        all_own(h).start()

        def push(d, inner):
            all_copy(h, d).start()
            return inner

        lax.fori_loop(1, chips, push, 0)
        return carry

    lax.fori_loop(0, GROUP_HEADS, send_head, 0)

    frame_block, row_block, inside = decode(order_t)
    block_of = frame_block * nh + row_block
    code = iota(order_t.shape, 0) * tok + inside
    found = []
    for b in range(4):
        mine = block_of == (2 * kk + b // 2) * nh + 2 * zz + b % 2
        found.append(jnp.min(jnp.where(mine, code, tok * tok), axis=0, keepdims=True) % tok)
        found.append(jnp.max(jnp.where(mine, code, 0), axis=0, keepdims=True) % tok)
    table = jnp.concatenate(found, axis=0).astype(F32).astype(BF16)
    rows = 4 * tok
    number = iota((nt * nh, rows), 1)
    from_chip, place_in = number // 16, number % 16
    sender = (from_chip // nh) * 2 * nh + ((place_in // 2) % 2) * nh + from_chip % nh
    spread = jnp.where(iota((nt * nh, rows), 0) == sender, 1.0, 0.0).astype(BF16)
    wide = dot(table, spread)
    lane = iota((8, rows), 1) % 16
    chosen = iota((8, rows), 0) == (lane // 4) * 2 + lane % 2
    position = jnp.sum(jnp.where(chosen, wide, 0.0), axis=0, keepdims=True).astype(jnp.int32)
    position = position + (iota((1, rows), 1) % 16 // 4) * tok

    def fill_place(b, carry):
        place[b] = jnp.where(iota((tok, rows), 0) + b * tok == position, 1.0, 0.0).astype(BF16)
        return carry

    lax.fori_loop(0, 4, fill_place, 0)

    pltpu.make_async_copy(
        grad_ref.at[:, group_cols((core, half))], grad_blocks.at[own_block], grad_sem
    ).wait()
    for n in range(3):
        grad_copy(n).wait_recv()

    def turn_grad(b, carry):
        for h in range(GROUP_HEADS):
            piece = grad_blocks[b, :, h * HEAD_DIM : (h + 1) * HEAD_DIM]
            grad_t[h, b] = piece.astype(F32).T.astype(BF16)
        return carry

    lax.fori_loop(0, 4, turn_grad, 0)

    def halo_copy(h, n):
        dk, dz = DIRECTIONS[n]
        return pltpu.make_async_remote_copy(
            src_ref=ext.at[h, own_part(dk), own_part(dz)],
            dst_ref=ext.at[h, halo_part(-dk), halo_part(-dz)],
            send_sem=halo_send_sem.at[h, n],
            recv_sem=halo_recv_sem.at[h, n],
            device_id=(ta + 2 * dk, ha + 2 * dz),
            device_id_type=MESH,
        )

    def back_copy(h, n):
        dk, dz = DIRECTIONS[n]
        return pltpu.make_async_remote_copy(
            src_ref=back_send.at[h, halo_part(dk), halo_part(dz)],
            dst_ref=back_recv.at[h, halo_part(-dk), halo_part(-dz)],
            send_sem=back_send_sem.at[h, n],
            recv_sem=back_recv_sem.at[h, n],
            device_id=(ta + 2 * dk, ha + 2 * dz),
            device_id_type=MESH,
        )

    def each_sent(step):
        for n, (dk, dz) in enumerate(DIRECTIONS):
            pl.when(exists(dk, dz))(functools.partial(step, n))

    def each_arrival(step):
        for n, (dk, dz) in enumerate(DIRECTIONS):
            pl.when(exists(-dk, -dz))(functools.partial(step, n))

    def gather_in(h, carry):
        all_own(h).wait()
        many = pl.ds(0, 16 * (chips - 1))
        pltpu.make_async_copy(recv.at[h, many], recv.at[h, many], all_recv_sem.at[h]).wait()
        return carry

    lax.fori_loop(0, GROUP_HEADS, gather_in, 0)

    def settle(h, carry):
        def one_block(b, inner):
            grid_rows = dot(place[b], recv[h])
            query_t[h, b] = grid_rows[:, :HEAD_DIM].T.astype(BF16)
            ext[h, 1 + b // 2, 1 + b % 2] = grid_rows[:, HEAD_DIM:].astype(BF16)
            return inner

        lax.fori_loop(0, 4, one_block, 0)
        each_sent(lambda n: halo_copy(h, n).start())
        return carry

    lax.fori_loop(0, GROUP_HEADS, settle, 0)

    outs = (att_ref, dq_ref, dk_ref, dv_ref)

    def out_cols(h):
        first = ((2 * core + half) * GROUP_HEADS + h) * HEAD_DIM
        return pl.ds(pl.multiple_of(first, HEAD_DIM), HEAD_DIM)

    def out_copy(o, h, n):
        return pltpu.make_async_remote_copy(
            src_ref=stage.at[o, h, 2 * others[n][0] + others[n][1]],
            dst_ref=outs[o].at[:, out_cols(h)],
            send_sem=out_send_sem.at[o],
            recv_sem=out_recv_sem.at[o],
            device_id=mate(others[n]),
            device_id_type=MESH,
        )

    def out_own(o, h):
        return pltpu.make_async_copy(
            stage.at[o, h, own_block], outs[o].at[:, out_cols(h)], out_sem.at[o]
        )

    def hand_out(o, h):
        for n in range(3):
            out_copy(o, h, n).start()
        out_own(o, h).start()

    def attend(h, carry):
        each_arrival(lambda n: halo_copy(h, n).wait_recv())

        def prepare(e, inner):
            ext_t[e // 4, e % 4] = ext[h, e // 4, e % 4].astype(F32).T.astype(BF16)
            acc[e // 4, e % 4] = jnp.zeros((tok, 2 * HEAD_DIM), F32)
            return inner

        lax.fori_loop(0, 16, prepare, 0)

        def one_block(b, inner):
            bi, bj = b // 2, b % 2
            q_t, g_t = query_t[h, b], grad_t[h, b]
            spots = [(bi + di, bj + dj) for di in range(3) for dj in range(3)]
            biases = []
            for i, j in spots:
                missing = (
                    ((kk == 0) & (i == 0))
                    | ((kk == nk - 1) & (i == 3))
                    | ((zz == 0) & (j == 0))
                    | ((zz == nz - 1) & (j == 3))
                )
                biases.append(jnp.where(missing, NEG, 0.0).astype(F32))
            top = jnp.full((1, tok), NEG, F32)
            for n, (i, j) in enumerate(spots):
                s = dot(ext[h, i, j, :, :HEAD_DIM], q_t)
                score[n] = s
                top = jnp.maximum(top, jnp.max(s, axis=0, keepdims=True) + biases[n])
            shift = top * (SCALE * LOG2E)
            total = jnp.zeros((1, tok), F32)
            out_t = jnp.zeros((HEAD_DIM, tok), F32)
            for n, (i, j) in enumerate(spots):
                p = jnp.exp2(score[n] * (SCALE * LOG2E) - (shift - biases[n]))
                total = total + jnp.sum(p, axis=0, keepdims=True)
                p_low = p.astype(BF16)
                prob[n] = p_low
                out_t = out_t + dot(ext_t[i, j, HEAD_DIM:, :], p_low)
            inverse = 1.0 / total
            out_t = out_t * inverse
            grad_f = g_t.astype(F32)
            delta = jnp.sum(grad_f * out_t, axis=0, keepdims=True)
            stage[0, h, b] = out_t.T.astype(BF16)
            g_scaled = (grad_f * inverse).astype(BF16)
            q_scaled = (q_t.astype(F32) * (inverse * SCALE)).astype(BF16)
            dq_t = jnp.zeros((HEAD_DIM, tok), F32)
            for n, (i, j) in enumerate(spots):
                dp = dot(ext[h, i, j, :, HEAD_DIM:], g_t)
                p_low = prob[n]
                ds = (p_low.astype(F32) * (dp - delta)).astype(BF16)
                dq_t = dq_t + dot(ext_t[i, j, :HEAD_DIM, :], ds)
                acc[i, j, :, :HEAD_DIM] += dot_nt(ds, q_scaled)
                acc[i, j, :, HEAD_DIM:] += dot_nt(p_low, g_scaled)
            stage[1, h, b] = (dq_t * (inverse * SCALE)).T.astype(BF16)
            return inner

        lax.fori_loop(0, 4, one_block, 0)

        def put_back(e, inner):
            back_send[h, e // 4, e % 4] = acc[e // 4, e % 4].astype(BF16)
            return inner

        lax.fori_loop(0, 16, put_back, 0)
        each_sent(lambda n: back_copy(h, n).start())
        hand_out(0, h)
        hand_out(1, h)

        def keep(b, inner):
            own_acc[h, b] = acc[1 + b // 2, 1 + b % 2]
            return inner

        lax.fori_loop(0, 4, keep, 0)
        return carry

    lax.fori_loop(0, GROUP_HEADS, attend, 0)

    def finish(h, carry):
        each_arrival(lambda n: back_copy(h, n).wait_recv())

        def one_block(b, inner):
            bi, bj = b // 2, b % 2
            far_i, far_j = 3 * bi, 3 * bj
            total = own_acc[h, b]
            for i, j in ((far_i, 1 + bj), (1 + bi, far_j), (far_i, far_j)):
                total = total + back_recv[h, i, j].astype(F32)
            low = total.astype(BF16)
            stage[2, h, b] = low[:, :HEAD_DIM]
            stage[3, h, b] = low[:, HEAD_DIM:]
            return inner

        lax.fori_loop(0, 4, one_block, 0)
        hand_out(2, h)
        hand_out(3, h)
        return carry

    lax.fori_loop(0, GROUP_HEADS, finish, 0)

    for a in range(3):
        pair_copy(a).wait_send()
    for n in range(3):
        grad_copy(n).wait_send()

    def sent(h, carry):
        many = pl.ds(0, 16 * (chips - 1))
        pltpu.make_async_copy(recv.at[h, many], recv.at[h, many], all_send_sem.at[h]).wait()
        each_sent(lambda n: halo_copy(h, n).wait_send())
        each_sent(lambda n: back_copy(h, n).wait_send())
        return carry

    lax.fori_loop(0, GROUP_HEADS, sent, 0)
    for o in range(4):
        mine = outs[o].at[:, pl.ds(0, width)]
        far = outs[o].at[:, pl.ds(0, 3 * width)]
        pltpu.make_async_copy(mine, mine, out_sem.at[o]).wait()
        pltpu.make_async_copy(far, far, out_send_sem.at[o]).wait()
        pltpu.make_async_copy(far, far, out_recv_sem.at[o]).wait()


def shards(nt, nh, query_seq, key_seq, value_seq, tile_order, grad_output):
    block_shape = grad_output.shape
    cols = block_shape[2]
    tok, channels = query_seq.shape
    low = jax.ShapeDtypeStruct((tok, channels), BF16)
    hbm = pl.BlockSpec(memory_space=pl.ANY)
    vmem = pl.BlockSpec(memory_space=pltpu.VMEM)
    gh, d = GROUP_HEADS, HEAD_DIM
    dma = pltpu.SemaphoreType.DMA
    outs = pl.pallas_call(
        functools.partial(kernel, nt, nh, cols),
        out_shape=[low] * 4,
        in_specs=[hbm, hbm, hbm, vmem, hbm],
        out_specs=[hbm] * 4,
        scratch_shapes=[
            pltpu.VMEM((3, 2 * tok, 2 * gh * d), BF16),
            pltpu.VMEM((2 * tok, 2 * tok), BF16),
            pltpu.VMEM((gh, 2, 2 * tok, 3 * d), BF16),
            pltpu.VMEM((gh, 4 * tok, 3 * d), BF16),
            pltpu.VMEM((4, tok, 4 * tok), BF16),
            pltpu.VMEM((gh, 4, 4, tok, 2 * d), BF16),
            pltpu.VMEM((4, 4, 2 * d, tok), BF16),
            pltpu.VMEM((gh, 4, d, tok), BF16),
            pltpu.VMEM((4, tok, gh * d), BF16),
            pltpu.VMEM((gh, 4, d, tok), BF16),
            pltpu.VMEM((9, tok, tok), F32),
            pltpu.VMEM((9, tok, tok), BF16),
            pltpu.VMEM((4, 4, tok, 2 * d), F32),
            pltpu.VMEM((gh, 4, tok, 2 * d), F32),
            pltpu.VMEM((gh, 4, 4, tok, 2 * d), BF16),
            pltpu.VMEM((gh, 4, 4, tok, 2 * d), BF16),
            pltpu.VMEM((4, gh, 4, tok, d), BF16),
            dma((3,)), dma((3,)), dma((3,)),
            dma, dma((3,)), dma((3,)),
            dma((gh,)), dma((gh,)), dma((gh,)),
            dma((gh, 8)), dma((gh, 8)), dma((gh, 8)), dma((gh, 8)),
            dma((4,)), dma((4,)), dma((4,)),
        ],
        compiler_params=pltpu.CompilerParams(
            collective_id=0, has_side_effects=True, vmem_limit_bytes=60 * 2**20
        ),
        cost_estimate=pl.CostEstimate(
            flops=12 * 4 * gh * 9 * tok * tok * d,
            bytes_accessed=16 * tok * channels,
            transcendentals=4 * gh * 9 * tok * tok,
        ),
    )(query_seq, key_seq, value_seq, tile_order.reshape(nt * nh, tok), grad_output.reshape(tok, channels))
    return tuple(o.reshape(block_shape) for o in outs)


def solution(mesh):
    seq = P(("ta", "ha"), None)
    grid = P("ta", "ha", None, None)
    return jax.shard_map(
        functools.partial(shards, mesh.shape["ta"], mesh.shape["ha"]),
        mesh=mesh,
        in_specs=(seq, seq, seq, P(), grid),
        out_specs=(grid,) * 4,
        check_vma=False,
    )
```

```python
import functools

import jax
import jax.numpy as jnp
from jax import lax
from jax.experimental import pallas as pl
from jax.experimental.pallas import tpu as pltpu
from jax.sharding import PartitionSpec as P

HEADS = 12
HEAD_DIM = 128
GROUP_HEADS = 3
TILE_FRAMES = 4
TILE_ROWS = 8
SCALE = HEAD_DIM ** (-0.5)
LOG2E = 1.4426950408889634
NEG = -1e30
MESH = pl.DeviceIdType.MESH
F32 = jnp.float32
BF16 = jnp.bfloat16
SEAT = {0: 0, 3: 1, 1: 2, 2: 3}


def dot(a, b):
    return jnp.dot(a, b, preferred_element_type=F32)


def dot_nt(a, b):
    return lax.dot_general(a, b, (((1,), (1,)), ((), ())), preferred_element_type=F32)


def iota(shape, dim):
    return lax.broadcasted_iota(jnp.int32, shape, dim)


def spots_of(b):
    return [(b // 2 + di, b % 2 + dj) for di in range(3) for dj in range(3)]


def kernel(
    nt, nh, cols,
    q_ref, k_ref, v_ref, order_ref, grad_ref,
    out_ref,
    pair, sort_one, send, recv, place, ext, ext_t, query_t, grad_blocks, grad_t,
    score, prob, grad_score, query_s, grad_s, keep,
    back_z, from_z, back_x, from_x, stage,
    pair_sem, pair_send_sem, pair_recv_sem,
    grad_sem, grad_send_sem, grad_recv_sem,
    all_sem, all_send_sem, all_recv_sem,
    side_send_sem, side_recv_sem, corner_send_sem, corner_recv_sem,
    back_z_send_sem, back_z_recv_sem, back_x_send_sem, back_x_recv_sem,
    out_sem, out_send_sem, out_recv_sem,
):
    tok = TILE_FRAMES * TILE_ROWS * cols
    nk, nz = nt // 2, nh // 2
    chips = nk * nh
    width = GROUP_HEADS * HEAD_DIM
    ta, ha = lax.axis_index("ta"), lax.axis_index("ha")
    kk, core = ta // 2, ta % 2
    zz, half = ha // 2, ha % 2
    chip = kk * nh + ha
    others = [(1 - core, half), (core, 1 - half), (1 - core, 1 - half)]

    def mate(where):
        return (2 * kk + where[0], 2 * zz + where[1])

    have_x = (kk > 0, kk < nk - 1)
    have_z = (zz > 0, zz < nz - 1)

    nothing = jnp.zeros((tok, 2 * HEAD_DIM), BF16)
    for side in range(2):

        @pl.when(jnp.logical_not(have_x[side]))
        def _(side=side):
            def clear(h, carry):
                for n in range(4):
                    ext[h, 3 * side, n] = nothing
                for n in range(2):
                    from_x[h, side, n] = nothing
                return carry

            lax.fori_loop(0, GROUP_HEADS, clear, 0)

        @pl.when(jnp.logical_not(have_z[side]))
        def _(side=side):
            def clear(h, carry):
                for n in range(4):
                    ext[h, n, 3 * side] = nothing
                    from_z[h, side, n] = nothing
                return carry

            lax.fori_loop(0, GROUP_HEADS, clear, 0)

    barrier = pltpu.get_barrier_semaphore()

    def greet(d, carry):
        to = lax.rem(chip + d, chips)
        pl.semaphore_signal(
            barrier, inc=1, device_id=(2 * (to // nh) + core, to % nh), device_id_type=MESH
        )
        return carry

    lax.fori_loop(1, chips, greet, 0)
    for where in ((1 - core, half), (1 - core, 1 - half)):
        pl.semaphore_signal(barrier, inc=1, device_id=mate(where), device_id_type=MESH)

    seq = (q_ref, k_ref, v_ref)
    pair_width = 2 * width
    own_cols = pl.ds(pl.multiple_of(core * pair_width, pair_width), pair_width)
    far_cols = pl.ds(pl.multiple_of((1 - core) * pair_width, pair_width), pair_width)
    own_rows = pl.ds(pl.multiple_of(core * tok, tok), tok)
    for a in range(3):
        pltpu.make_async_copy(
            seq[a].at[:, own_cols], pair.at[a, own_rows], pair_sem.at[a]
        ).start()

    def group_cols(where, n=width):
        return pl.ds(pl.multiple_of((2 * where[0] + where[1]) * width, width), width)

    own_block = 2 * core + half
    pltpu.make_async_copy(
        grad_ref.at[:, group_cols((core, half))], grad_blocks.at[own_block], grad_sem
    ).start()

    pl.semaphore_wait(barrier, chips + 1)

    def pair_copy(a):
        return pltpu.make_async_remote_copy(
            src_ref=seq[a].at[:, far_cols],
            dst_ref=pair.at[a, own_rows],
            send_sem=pair_send_sem.at[a],
            recv_sem=pair_recv_sem.at[a],
            device_id=mate((1 - core, half)),
            device_id_type=MESH,
        )

    def grad_copy(n):
        return pltpu.make_async_remote_copy(
            src_ref=grad_ref.at[:, group_cols(others[n])],
            dst_ref=grad_blocks.at[own_block],
            send_sem=grad_send_sem.at[n],
            recv_sem=grad_recv_sem.at[n],
            device_id=mate(others[n]),
            device_id_type=MESH,
        )

    for a in range(3):
        pair_copy(a).start()
    for n in range(3):
        grad_copy(n).start()

    def decode(t):
        frame = t // (nh * TILE_ROWS * cols)
        row = (t // cols) % (nh * TILE_ROWS)
        frame_block, row_block = frame // TILE_FRAMES, row // TILE_ROWS
        inside = ((frame % TILE_FRAMES) * TILE_ROWS + row % TILE_ROWS) * cols + t % cols
        return frame_block, row_block, inside

    order = order_ref[...]
    order_t = order.T
    for cc in range(2):
        source = kk * 2 * nh + cc * nh + ha
        line = order_ref[pl.ds(source, 1), :]
        column = jnp.sum(
            jnp.where(iota(order_t.shape, 1) == source, order_t, 0), axis=1, keepdims=True
        )
        line_f, line_r, _ = decode(line)
        col_f, col_r, _ = decode(column)
        same = (line_f * nh + line_r) == (col_f * nh + col_r)
        earlier = iota((tok, tok), 0) < iota((tok, tok), 1)
        second = jnp.sum(jnp.where(same & earlier, 1, 0), axis=0, keepdims=True)
        region = (line_f // 2) * nz + line_r // 2
        seat = region * 16 + ((line_f % 2) * 2 + line_r % 2) * 4 + cc * 2 + second
        sort_one[:, cc * tok : (cc + 1) * tok] = jnp.where(
            iota((2 * tok, tok), 0) == seat, 1.0, 0.0
        ).astype(BF16)

    for a in range(3):
        pltpu.make_async_copy(
            seq[a].at[:, own_cols], pair.at[a, own_rows], pair_sem.at[a]
        ).wait()
        pair_copy(a).wait_recv()

    def all_copy(h, d):
        to = lax.rem(chip + d, chips)
        to_k, to_h = to // nh, to % nh
        region = to_k * nz + to_h // 2
        return pltpu.make_async_remote_copy(
            src_ref=send.at[h, to_h % 2, pl.ds(pl.multiple_of(region * 16, 16), 16)],
            dst_ref=recv.at[h, pl.ds(pl.multiple_of(chip * 16, 16), 16)],
            send_sem=all_send_sem.at[h],
            recv_sem=all_recv_sem.at[h],
            device_id=(2 * to_k + core, to_h),
            device_id_type=MESH,
        )

    def all_own(h):
        region = kk * nz + zz
        return pltpu.make_async_copy(
            send.at[h, half, pl.ds(pl.multiple_of(region * 16, 16), 16)],
            recv.at[h, pl.ds(pl.multiple_of(chip * 16, 16), 16)],
            all_sem.at[h],
        )

    def send_head(h, carry):
        for a in range(3):
            left = pl.ds(pl.multiple_of(h * HEAD_DIM, HEAD_DIM), HEAD_DIM)
            right = pl.ds(pl.multiple_of(width + h * HEAD_DIM, HEAD_DIM), HEAD_DIM)
            both = jnp.concatenate([pair[a, :, left], pair[a, :, right]], axis=1)
            sorted_rows = dot(sort_one[...], both).astype(BF16)
            into = slice(a * HEAD_DIM, (a + 1) * HEAD_DIM)
            send[h, 0, :, into] = sorted_rows[:, :HEAD_DIM]
            send[h, 1, :, into] = sorted_rows[:, HEAD_DIM:]
        all_own(h).start()

        def push(d, inner):
            all_copy(h, d).start()
            return inner

        lax.fori_loop(1, chips, push, 0)
        return carry

    lax.fori_loop(0, GROUP_HEADS, send_head, 0)

    frame_block, row_block, inside = decode(order_t)
    block_of = frame_block * nh + row_block
    code = iota(order_t.shape, 0) * tok + inside
    found = []
    for b in range(4):
        mine = block_of == (2 * kk + b // 2) * nh + 2 * zz + b % 2
        found.append(jnp.min(jnp.where(mine, code, tok * tok), axis=0, keepdims=True) % tok)
        found.append(jnp.max(jnp.where(mine, code, 0), axis=0, keepdims=True) % tok)
    table = jnp.concatenate(found, axis=0).astype(F32).astype(BF16)
    rows = 4 * tok
    number = iota((nt * nh, rows), 1)
    from_chip, place_in = number // 16, number % 16
    sender = (from_chip // nh) * 2 * nh + ((place_in // 2) % 2) * nh + from_chip % nh
    spread = jnp.where(iota((nt * nh, rows), 0) == sender, 1.0, 0.0).astype(BF16)
    wide = dot(table, spread)
    lane = iota((8, rows), 1) % 16
    chosen = iota((8, rows), 0) == (lane // 4) * 2 + lane % 2
    position = jnp.sum(jnp.where(chosen, wide, 0.0), axis=0, keepdims=True).astype(jnp.int32)
    position = position + (iota((1, rows), 1) % 16 // 4) * tok

    def fill_place(b, carry):
        place[b] = jnp.where(iota((tok, rows), 0) + b * tok == position, 1.0, 0.0).astype(BF16)
        return carry

    lax.fori_loop(0, 4, fill_place, 0)

    pltpu.make_async_copy(
        grad_ref.at[:, group_cols((core, half))], grad_blocks.at[own_block], grad_sem
    ).wait()
    for n in range(3):
        grad_copy(n).wait_recv()

    def turn_grad(b, carry):
        for h in range(GROUP_HEADS):
            piece = grad_blocks[b, :, h * HEAD_DIM : (h + 1) * HEAD_DIM]
            grad_t[h, b] = piece.astype(F32).T.astype(BF16)
        return carry

    lax.fori_loop(0, 4, turn_grad, 0)

    def x_device(side):
        return (ta + 2 * (2 * side - 1), ha)

    def z_device(side):
        return (ta, ha + 2 * (2 * side - 1))

    def remote(src, dst, sends, recvs, index, device):
        return pltpu.make_async_remote_copy(
            src_ref=src, dst_ref=dst, send_sem=sends.at[index], recv_sem=recvs.at[index],
            device_id=device, device_id_type=MESH,
        )

    def x_side(h, side):
        return remote(
            ext.at[h, 1 + side, pl.ds(1, 2)], ext.at[h, 3 - 3 * side, pl.ds(1, 2)],
            side_send_sem, side_recv_sem, (h, side), x_device(side),
        )

    def z_side(h, side):
        return remote(
            ext.at[h, pl.ds(1, 2), 1 + side], ext.at[h, pl.ds(1, 2), 3 - 3 * side],
            side_send_sem, side_recv_sem, (h, 2 + side), z_device(side),
        )

    def corner(h, column, side):
        return remote(
            ext.at[h, 3 * column, 1 + side], ext.at[h, 3 * column, 3 - 3 * side],
            corner_send_sem, corner_recv_sem, (h, 2 * column + side), z_device(side),
        )

    def z_back(h, side, kind):
        return remote(
            back_z.at[h, side, pl.ds(2 * kind, 2)], from_z.at[h, 1 - side, pl.ds(2 * kind, 2)],
            back_z_send_sem, back_z_recv_sem, (h, 2 * side + kind), z_device(side),
        )

    def x_back(h, side):
        return remote(
            back_x.at[h, side], from_x.at[h, 1 - side],
            back_x_send_sem, back_x_recv_sem, (h, side), x_device(side),
        )

    def along(have, step):
        for side in range(2):
            pl.when(have[side])(functools.partial(step, side))

    def corners(have, step):
        for column in range(2):
            for side in range(2):
                pl.when(have_x[column] & have[side])(functools.partial(step, column, side))

    came_x, came_z = have_x[::-1], have_z[::-1]

    def gather_in(h, carry):
        all_own(h).wait()
        many = pl.ds(0, 16 * (chips - 1))
        pltpu.make_async_copy(recv.at[h, many], recv.at[h, many], all_recv_sem.at[h]).wait()
        return carry

    lax.fori_loop(0, GROUP_HEADS, gather_in, 0)

    def settle(h, carry):
        def one_block(b, inner):
            grid_rows = dot(place[b], recv[h])
            query_t[h, b] = grid_rows[:, :HEAD_DIM].T.astype(BF16)
            ext[h, 1 + b // 2, 1 + b % 2] = grid_rows[:, HEAD_DIM:].astype(BF16)
            return inner

        lax.fori_loop(0, 4, one_block, 0)
        along(have_x, lambda side: x_side(h, side).start())

        @pl.when(h == 0)
        def _():
            along(have_z, lambda side: z_side(h, side).start())

        return carry

    lax.fori_loop(0, GROUP_HEADS, settle, 0)

    def pass_corners(h):
        along(came_x, lambda side: x_side(h, side).wait_recv())
        corners(have_z, lambda column, side: corner(h, column, side).start())

    pass_corners(0)
    along(have_z, lambda side: z_side(1, side).start())
    pass_corners(1)
    along(have_z, lambda side: z_side(2, side).start())

    def out_cols(h):
        first = ((2 * core + half) * GROUP_HEADS + h) * HEAD_DIM
        return pl.ds(pl.multiple_of(first, HEAD_DIM), HEAD_DIM)

    def out_copy(pair_of, h, n):
        two = pl.ds(2 * pair_of, 2)
        return remote(
            stage.at[h, 2 * others[n][0] + others[n][1], two], out_ref.at[two, :, out_cols(h)],
            out_send_sem, out_recv_sem, pair_of, mate(others[n]),
        )

    def out_own(pair_of, h):
        two = pl.ds(2 * pair_of, 2)
        return pltpu.make_async_copy(
            stage.at[h, own_block, two], out_ref.at[two, :, out_cols(h)], out_sem.at[pair_of]
        )

    def hand_out(pair_of, h):
        for n in (1, 2, 0):
            out_copy(pair_of, h, n).start()
        out_own(pair_of, h).start()

    def bias_of(i, j):
        gone = [jnp.logical_not(have_x[i // 3])] if i in (0, 3) else []
        gone += [jnp.logical_not(have_z[j // 3])] if j in (0, 3) else []
        if not gone:
            return None
        return jnp.where(functools.reduce(jnp.logical_or, gone), NEG, 0.0).astype(F32)

    bias = {(i, j): bias_of(i, j) for i in range(4) for j in range(4)}

    def attend(h, carry):
        along(came_z, lambda side: z_side(h, side).wait_recv())
        corners(came_z, lambda column, side: corner(h, column, side).wait_recv())

        def prepare(e, inner):
            ext_t[e // 4, e % 4] = ext[h, e // 4, e % 4].astype(F32).T.astype(BF16)
            return inner

        lax.fori_loop(0, 16, prepare, 0)
        top, total, out_t, dq_t = [None] * 4, [None] * 4, [None] * 4, [None] * 4
        delta, inverse = [None] * 4, [None] * 4

        def add(held, b, n, term):
            held[b] = term if n == 0 else held[b] + term

        def scores_of(b, n):
            spot = spots_of(b)[n]
            s = dot(ext[h, spot[0], spot[1], :, :HEAD_DIM], query_t[h, b])
            score[b % 2, n] = s
            most = jnp.max(s, axis=0, keepdims=True)
            if bias[spot] is not None:
                most = most + bias[spot]
            top[b] = most if n == 0 else jnp.maximum(top[b], most)

        def forward(b, n):
            i, j = spots_of(b)[n]
            shift = top[b] * (SCALE * LOG2E)
            if bias[i, j] is not None:
                shift = shift - bias[i, j]
            p = jnp.exp2(score[b % 2, n] * (SCALE * LOG2E) - shift)
            add(total, b, n, jnp.sum(p, axis=0, keepdims=True))
            p_low = p.astype(BF16)
            prob[b, n] = p_low
            add(out_t, b, n, dot(ext_t[i, j, HEAD_DIM:, :], p_low))
            if n == 8:
                inverse[b] = 1.0 / total[b]
                full = out_t[b] * inverse[b]
                grad_f = grad_t[h, b].astype(F32)
                delta[b] = jnp.sum(grad_f * full, axis=0, keepdims=True)
                stage[h, b, 0] = full.T.astype(BF16)
                grad_s[b] = (grad_f * inverse[b]).astype(BF16)
                query_s[b] = (query_t[h, b].astype(F32) * (inverse[b] * SCALE)).astype(BF16)

        def backward(b, n):
            i, j = spots_of(b)[n]
            dp = dot(ext[h, i, j, :, HEAD_DIM:], grad_t[h, b])
            ds = (prob[b, n].astype(F32) * (dp - delta[b])).astype(BF16)
            grad_score[b, n] = ds
            add(dq_t, b, n, dot(ext_t[i, j, :HEAD_DIM, :], ds))
            if n == 8:
                stage[h, b, 1] = (dq_t[b] * (inverse[b] * SCALE)).T.astype(BF16)

        for turn in range(6):
            for n in range(9):
                for step, b in ((scores_of, turn), (forward, turn - 1), (backward, turn - 2)):
                    if 0 <= b < 4:
                        step(b, n)

        def key_terms(i, j):
            k_sum = v_sum = None
            for b in range(4):
                if (i, j) in spots_of(b):
                    n = spots_of(b).index((i, j))
                    k_term = dot_nt(grad_score[b, n], query_s[b])
                    v_term = dot_nt(prob[b, n], grad_s[b])
                    k_sum = k_term if k_sum is None else k_sum + k_term
                    v_sum = v_term if v_sum is None else v_sum + v_term
            return ((slice(0, HEAD_DIM), k_sum), (slice(HEAD_DIM, 2 * HEAD_DIM), v_sum))

        for kind in range(2):
            for side in range(2):
                for i in ((0, 3), (1, 2))[kind]:
                    for lanes, value in key_terms(i, 3 * side):
                        back_z[h, side, SEAT[i], :, lanes] = value.astype(BF16)
            along(have_z, lambda side: z_back(h, side, kind).start())
        hand_out(0, h)
        for i in (0, 3, 1, 2):
            for j in (1, 2):
                for lanes, value in key_terms(i, j):
                    keep[h, i, j - 1, :, lanes] = value
        return carry

    def turn_x(h):
        along(came_z, lambda side: z_back(h, side, 0).wait_recv())
        for side in range(2):
            for j in range(2):
                both = keep[h, 3 * side, j] + from_z[h, j, side].astype(F32)
                back_x[h, side, j] = both.astype(BF16)
        along(have_x, lambda side: x_back(h, side).start())

    def heads(h, carry):
        attend(h, 0)

        @pl.when(h == 0)
        def _():
            pass_corners(GROUP_HEADS - 1)

        @pl.when(h > 0)
        def _():
            turn_x(h - 1)

        return carry

    lax.fori_loop(0, GROUP_HEADS, heads, 0)
    turn_x(GROUP_HEADS - 1)

    def finish(h, carry):
        along(came_z, lambda side: z_back(h, side, 1).wait_recv())
        along(came_x, lambda side: x_back(h, side).wait_recv())
        for b in range(4):
            i, j = b // 2, b % 2
            whole = keep[h, 1 + i, j] + from_z[h, j, 2 + i].astype(F32)
            low = (whole + from_x[h, i, j].astype(F32)).astype(BF16)
            stage[h, b, 2] = low[:, :HEAD_DIM]
            stage[h, b, 3] = low[:, HEAD_DIM:]
        hand_out(1, h)
        return carry

    lax.fori_loop(0, GROUP_HEADS, finish, 0)

    for a in range(3):
        pair_copy(a).wait_send()
    for n in range(3):
        grad_copy(n).wait_send()

    def sent(h, carry):
        many = pl.ds(0, 16 * (chips - 1))
        pltpu.make_async_copy(recv.at[h, many], recv.at[h, many], all_send_sem.at[h]).wait()
        along(have_x, lambda side: x_side(h, side).wait_send())
        along(have_z, lambda side: z_side(h, side).wait_send())
        corners(have_z, lambda column, side: corner(h, column, side).wait_send())
        for kind in range(2):
            along(have_z, lambda side: z_back(h, side, kind).wait_send())
        along(have_x, lambda side: x_back(h, side).wait_send())
        return carry

    lax.fori_loop(0, GROUP_HEADS, sent, 0)
    for pair_of in range(2):
        two = pl.ds(2 * pair_of, 2)
        mine = out_ref.at[two, :, pl.ds(0, width)]
        far = out_ref.at[two, :, pl.ds(0, 3 * width)]
        pltpu.make_async_copy(mine, mine, out_sem.at[pair_of]).wait()
        pltpu.make_async_copy(far, far, out_send_sem.at[pair_of]).wait()
        pltpu.make_async_copy(far, far, out_recv_sem.at[pair_of]).wait()


def deal(in_ref, *refs):
    outs, sems = refs[:4], refs[4]
    copies = [pltpu.make_async_copy(in_ref.at[n], outs[n], sems.at[n]) for n in range(4)]
    for copy in copies:
        copy.start()
    for copy in copies:
        copy.wait()


def shards(nt, nh, query_seq, key_seq, value_seq, tile_order, grad_output):
    block_shape = grad_output.shape
    cols = block_shape[2]
    tok, channels = query_seq.shape
    low = jax.ShapeDtypeStruct((tok, channels), BF16)
    hbm = pl.BlockSpec(memory_space=pl.ANY)
    vmem = pl.BlockSpec(memory_space=pltpu.VMEM)
    gh, d = GROUP_HEADS, HEAD_DIM
    dma = pltpu.SemaphoreType.DMA
    whole = pl.pallas_call(
        functools.partial(kernel, nt, nh, cols),
        out_shape=jax.ShapeDtypeStruct((4, tok, channels), BF16),
        in_specs=[hbm, hbm, hbm, vmem, hbm],
        out_specs=hbm,
        scratch_shapes=[
            pltpu.VMEM((3, 2 * tok, 2 * gh * d), BF16),
            pltpu.VMEM((2 * tok, 2 * tok), BF16),
            pltpu.VMEM((gh, 2, 2 * tok, 3 * d), BF16),
            pltpu.VMEM((gh, 4 * tok, 3 * d), BF16),
            pltpu.VMEM((4, tok, 4 * tok), BF16),
            pltpu.VMEM((gh, 4, 4, tok, 2 * d), BF16),
            pltpu.VMEM((4, 4, 2 * d, tok), BF16),
            pltpu.VMEM((gh, 4, d, tok), BF16),
            pltpu.VMEM((4, tok, gh * d), BF16),
            pltpu.VMEM((gh, 4, d, tok), BF16),
            pltpu.VMEM((2, 9, tok, tok), F32),
            pltpu.VMEM((4, 9, tok, tok), BF16),
            pltpu.VMEM((4, 9, tok, tok), BF16),
            pltpu.VMEM((4, d, tok), BF16),
            pltpu.VMEM((4, d, tok), BF16),
            pltpu.VMEM((gh, 4, 2, tok, 2 * d), F32),
            pltpu.VMEM((gh, 2, 4, tok, 2 * d), BF16),
            pltpu.VMEM((gh, 2, 4, tok, 2 * d), BF16),
            pltpu.VMEM((gh, 2, 2, tok, 2 * d), BF16),
            pltpu.VMEM((gh, 2, 2, tok, 2 * d), BF16),
            pltpu.VMEM((gh, 4, 4, tok, d), BF16),
            dma((3,)), dma((3,)), dma((3,)),
            dma, dma((3,)), dma((3,)),
            dma((gh,)), dma((gh,)), dma((gh,)),
            dma((gh, 4)), dma((gh, 4)), dma((gh, 4)), dma((gh, 4)),
            dma((gh, 4)), dma((gh, 4)), dma((gh, 2)), dma((gh, 2)),
            dma((2,)), dma((2,)), dma((2,)),
        ],
        compiler_params=pltpu.CompilerParams(
            collective_id=0, has_side_effects=True, vmem_limit_bytes=60 * 2**20
        ),
        cost_estimate=pl.CostEstimate(
            flops=12 * 4 * gh * 9 * tok * tok * d,
            bytes_accessed=16 * tok * channels,
            transcendentals=4 * gh * 9 * tok * tok,
        ),
    )(query_seq, key_seq, value_seq, tile_order.reshape(nt * nh, tok), grad_output.reshape(tok, channels))
    outs = pl.pallas_call(
        deal,
        out_shape=[low] * 4,
        in_specs=[hbm],
        out_specs=[hbm] * 4,
        scratch_shapes=[dma((4,))],
    )(whole)
    return tuple(o.reshape(block_shape) for o in outs)


def solution(mesh):
    seq = P(("ta", "ha"), None)
    grid = P("ta", "ha", None, None)
    return jax.shard_map(
        functools.partial(shards, mesh.shape["ta"], mesh.shape["ha"]),
        mesh=mesh,
        in_specs=(seq, seq, seq, P(), grid),
        out_specs=(grid,) * 4,
        check_vma=False,
    )
```

```python
import functools

import jax
import jax.numpy as jnp
from jax import lax
from jax.experimental import pallas as pl
from jax.experimental.pallas import tpu as pltpu
from jax.sharding import PartitionSpec as P

HEADS = 12
HEAD_DIM = 128
GROUP_HEADS = 3
TILE_FRAMES = 4
TILE_ROWS = 8
SCALE = HEAD_DIM ** (-0.5)
LOG2E = 1.4426950408889634
NEG = -1e30
MESH = pl.DeviceIdType.MESH
F32 = jnp.float32
BF16 = jnp.bfloat16
SEAT = {0: 0, 3: 1, 1: 2, 2: 3}


def dot(a, b):
    return jnp.dot(a, b, preferred_element_type=F32)


def dot_nt(a, b):
    return lax.dot_general(a, b, (((1,), (1,)), ((), ())), preferred_element_type=F32)


def iota(shape, dim):
    return lax.broadcasted_iota(jnp.int32, shape, dim)


def spots_of(b):
    return [(b // 2 + di, b % 2 + dj) for di in range(3) for dj in range(3)]


def kernel(
    nt, nh, cols,
    q_ref, k_ref, v_ref, order_ref, grad_ref,
    out_ref,
    pair, sort_one, send, recv, place, ext, ext_t, query_t, grad_blocks, grad_t,
    score, prob, grad_score, query_s, grad_s, keep,
    back_z, from_z, back_x, from_x, stage,
    pair_sem, pair_send_sem, pair_recv_sem,
    grad_sem, grad_send_sem, grad_recv_sem,
    all_sem, all_send_sem, all_recv_sem,
    side_send_sem, side_recv_sem, corner_send_sem, corner_recv_sem,
    back_z_send_sem, back_z_recv_sem, back_x_send_sem, back_x_recv_sem,
    out_sem, out_send_sem, out_recv_sem,
):
    tok = TILE_FRAMES * TILE_ROWS * cols
    nk, nz = nt // 2, nh // 2
    chips = nk * nh
    width = GROUP_HEADS * HEAD_DIM
    ta, ha = lax.axis_index("ta"), lax.axis_index("ha")
    kk, core = ta // 2, ta % 2
    zz, half = ha // 2, ha % 2
    chip = kk * nh + ha
    others = [(1 - core, half), (core, 1 - half), (1 - core, 1 - half)]

    def mate(where):
        return (2 * kk + where[0], 2 * zz + where[1])

    have_x = (kk > 0, kk < nk - 1)
    have_z = (zz > 0, zz < nz - 1)

    nothing = jnp.zeros((tok, 2 * HEAD_DIM), BF16)
    for side in range(2):

        @pl.when(jnp.logical_not(have_x[side]))
        def _(side=side):
            def clear(h, carry):
                for n in range(4):
                    ext[h, 3 * side, n] = nothing
                for n in range(2):
                    from_x[h, side, n] = nothing
                return carry

            lax.fori_loop(0, GROUP_HEADS, clear, 0)

        @pl.when(jnp.logical_not(have_z[side]))
        def _(side=side):
            def clear(h, carry):
                for n in range(4):
                    ext[h, n, 3 * side] = nothing
                    from_z[h, side, n] = nothing
                return carry

            lax.fori_loop(0, GROUP_HEADS, clear, 0)

    barrier = pltpu.get_barrier_semaphore()

    def greet(d, carry):
        to = lax.rem(chip + d, chips)
        pl.semaphore_signal(
            barrier, inc=1, device_id=(2 * (to // nh) + core, to % nh), device_id_type=MESH
        )
        return carry

    lax.fori_loop(1, chips, greet, 0)
    for where in ((1 - core, half), (1 - core, 1 - half)):
        pl.semaphore_signal(barrier, inc=1, device_id=mate(where), device_id_type=MESH)

    seq = (q_ref, k_ref, v_ref)
    pair_width = 2 * width
    own_cols = pl.ds(pl.multiple_of(core * pair_width, pair_width), pair_width)
    far_cols = pl.ds(pl.multiple_of((1 - core) * pair_width, pair_width), pair_width)
    own_rows = pl.ds(pl.multiple_of(core * tok, tok), tok)
    for a in range(3):
        pltpu.make_async_copy(
            seq[a].at[:, own_cols], pair.at[a, own_rows], pair_sem.at[a]
        ).start()

    def group_cols(where, n=width):
        return pl.ds(pl.multiple_of((2 * where[0] + where[1]) * width, width), width)

    own_block = 2 * core + half
    pltpu.make_async_copy(
        grad_ref.at[:, group_cols((core, half))], grad_blocks.at[own_block], grad_sem
    ).start()

    pl.semaphore_wait(barrier, chips + 1)

    def pair_copy(a):
        return pltpu.make_async_remote_copy(
            src_ref=seq[a].at[:, far_cols],
            dst_ref=pair.at[a, own_rows],
            send_sem=pair_send_sem.at[a],
            recv_sem=pair_recv_sem.at[a],
            device_id=mate((1 - core, half)),
            device_id_type=MESH,
        )

    def grad_copy(n):
        return pltpu.make_async_remote_copy(
            src_ref=grad_ref.at[:, group_cols(others[n])],
            dst_ref=grad_blocks.at[own_block],
            send_sem=grad_send_sem.at[n],
            recv_sem=grad_recv_sem.at[n],
            device_id=mate(others[n]),
            device_id_type=MESH,
        )

    for a in range(3):
        pair_copy(a).start()
    for n in range(3):
        grad_copy(n).start()

    def decode(t):
        frame = t // (nh * TILE_ROWS * cols)
        row = (t // cols) % (nh * TILE_ROWS)
        frame_block, row_block = frame // TILE_FRAMES, row // TILE_ROWS
        inside = ((frame % TILE_FRAMES) * TILE_ROWS + row % TILE_ROWS) * cols + t % cols
        return frame_block, row_block, inside

    order = order_ref[...]
    order_t = order.T
    for cc in range(2):
        source = kk * 2 * nh + cc * nh + ha
        line = order_ref[pl.ds(source, 1), :]
        column = jnp.sum(
            jnp.where(iota(order_t.shape, 1) == source, order_t, 0), axis=1, keepdims=True
        )
        line_f, line_r, _ = decode(line)
        col_f, col_r, _ = decode(column)
        same = (line_f * nh + line_r) == (col_f * nh + col_r)
        earlier = iota((tok, tok), 0) < iota((tok, tok), 1)
        second = jnp.sum(jnp.where(same & earlier, 1, 0), axis=0, keepdims=True)
        region = (line_f // 2) * nz + line_r // 2
        seat = region * 16 + ((line_f % 2) * 2 + line_r % 2) * 4 + cc * 2 + second
        sort_one[:, cc * tok : (cc + 1) * tok] = jnp.where(
            iota((2 * tok, tok), 0) == seat, 1.0, 0.0
        ).astype(BF16)

    for a in range(3):
        pltpu.make_async_copy(
            seq[a].at[:, own_cols], pair.at[a, own_rows], pair_sem.at[a]
        ).wait()
        pair_copy(a).wait_recv()

    def all_copy(h, d):
        to = lax.rem(chip + d, chips)
        to_k, to_h = to // nh, to % nh
        region = to_k * nz + to_h // 2
        return pltpu.make_async_remote_copy(
            src_ref=send.at[h, to_h % 2, pl.ds(pl.multiple_of(region * 16, 16), 16)],
            dst_ref=recv.at[h, pl.ds(pl.multiple_of(chip * 16, 16), 16)],
            send_sem=all_send_sem.at[h],
            recv_sem=all_recv_sem.at[h],
            device_id=(2 * to_k + core, to_h),
            device_id_type=MESH,
        )

    def all_own(h):
        region = kk * nz + zz
        return pltpu.make_async_copy(
            send.at[h, half, pl.ds(pl.multiple_of(region * 16, 16), 16)],
            recv.at[h, pl.ds(pl.multiple_of(chip * 16, 16), 16)],
            all_sem.at[h],
        )

    def send_head(h, carry):
        for a in range(3):
            left = pl.ds(pl.multiple_of(h * HEAD_DIM, HEAD_DIM), HEAD_DIM)
            right = pl.ds(pl.multiple_of(width + h * HEAD_DIM, HEAD_DIM), HEAD_DIM)
            both = jnp.concatenate([pair[a, :, left], pair[a, :, right]], axis=1)
            sorted_rows = dot(sort_one[...], both).astype(BF16)
            into = slice(a * HEAD_DIM, (a + 1) * HEAD_DIM)
            send[h, 0, :, into] = sorted_rows[:, :HEAD_DIM]
            send[h, 1, :, into] = sorted_rows[:, HEAD_DIM:]
        all_own(h).start()

        def push(d, inner):
            all_copy(h, d).start()
            return inner

        lax.fori_loop(1, chips, push, 0)
        return carry

    lax.fori_loop(0, GROUP_HEADS, send_head, 0)

    frame_block, row_block, inside = decode(order_t)
    block_of = frame_block * nh + row_block
    code = iota(order_t.shape, 0) * tok + inside
    found = []
    for b in range(4):
        mine = block_of == (2 * kk + b // 2) * nh + 2 * zz + b % 2
        found.append(jnp.min(jnp.where(mine, code, tok * tok), axis=0, keepdims=True) % tok)
        found.append(jnp.max(jnp.where(mine, code, 0), axis=0, keepdims=True) % tok)
    table = jnp.concatenate(found, axis=0).astype(F32).astype(BF16)
    rows = 4 * tok
    number = iota((nt * nh, rows), 1)
    from_chip, place_in = number // 16, number % 16
    sender = (from_chip // nh) * 2 * nh + ((place_in // 2) % 2) * nh + from_chip % nh
    spread = jnp.where(iota((nt * nh, rows), 0) == sender, 1.0, 0.0).astype(BF16)
    wide = dot(table, spread)
    lane = iota((8, rows), 1) % 16
    chosen = iota((8, rows), 0) == (lane // 4) * 2 + lane % 2
    position = jnp.sum(jnp.where(chosen, wide, 0.0), axis=0, keepdims=True).astype(jnp.int32)
    position = position + (iota((1, rows), 1) % 16 // 4) * tok

    def fill_place(b, carry):
        place[b] = jnp.where(iota((tok, rows), 0) + b * tok == position, 1.0, 0.0).astype(BF16)
        return carry

    lax.fori_loop(0, 4, fill_place, 0)

    pltpu.make_async_copy(
        grad_ref.at[:, group_cols((core, half))], grad_blocks.at[own_block], grad_sem
    ).wait()
    for n in range(3):
        grad_copy(n).wait_recv()

    def turn_grad(b, carry):
        for h in range(GROUP_HEADS):
            piece = grad_blocks[b, :, h * HEAD_DIM : (h + 1) * HEAD_DIM]
            grad_t[h, b] = piece.astype(F32).T.astype(BF16)
        return carry

    lax.fori_loop(0, 4, turn_grad, 0)

    def x_device(side):
        return (ta + 2 * (2 * side - 1), ha)

    def z_device(side):
        return (ta, ha + 2 * (2 * side - 1))

    def remote(src, dst, sends, recvs, index, device):
        return pltpu.make_async_remote_copy(
            src_ref=src, dst_ref=dst, send_sem=sends.at[index], recv_sem=recvs.at[index],
            device_id=device, device_id_type=MESH,
        )

    def x_side(h, side):
        return remote(
            ext.at[h, 1 + side, pl.ds(1, 2)], ext.at[h, 3 - 3 * side, pl.ds(1, 2)],
            side_send_sem, side_recv_sem, (h, side), x_device(side),
        )

    def z_side(h, side):
        return remote(
            ext.at[h, pl.ds(1, 2), 1 + side], ext.at[h, pl.ds(1, 2), 3 - 3 * side],
            side_send_sem, side_recv_sem, (h, 2 + side), z_device(side),
        )

    def corner(h, column, side):
        return remote(
            ext.at[h, 3 * column, 1 + side], ext.at[h, 3 * column, 3 - 3 * side],
            corner_send_sem, corner_recv_sem, (h, 2 * column + side), z_device(side),
        )

    def z_back(h, side, kind):
        return remote(
            back_z.at[h, side, pl.ds(2 * kind, 2)], from_z.at[h, 1 - side, pl.ds(2 * kind, 2)],
            back_z_send_sem, back_z_recv_sem, (h, 2 * side + kind), z_device(side),
        )

    def x_back(h, side):
        return remote(
            back_x.at[h, side], from_x.at[h, 1 - side],
            back_x_send_sem, back_x_recv_sem, (h, side), x_device(side),
        )

    def along(have, step):
        for side in range(2):
            pl.when(have[side])(functools.partial(step, side))

    def corners(have, step):
        for column in range(2):
            for side in range(2):
                pl.when(have_x[column] & have[side])(functools.partial(step, column, side))

    came_x, came_z = have_x[::-1], have_z[::-1]

    def gather_in(h, carry):
        all_own(h).wait()
        many = pl.ds(0, 16 * (chips - 1))
        pltpu.make_async_copy(recv.at[h, many], recv.at[h, many], all_recv_sem.at[h]).wait()
        return carry

    lax.fori_loop(0, GROUP_HEADS, gather_in, 0)

    def settle(h, carry):
        def one_block(b, inner):
            grid_rows = dot(place[b], recv[h])
            query_t[h, b] = grid_rows[:, :HEAD_DIM].T.astype(BF16)
            ext[h, 1 + b // 2, 1 + b % 2] = grid_rows[:, HEAD_DIM:].astype(BF16)
            return inner

        lax.fori_loop(0, 4, one_block, 0)
        along(have_x, lambda side: x_side(h, side).start())

        @pl.when(h == 0)
        def _():
            along(have_z, lambda side: z_side(h, side).start())

        return carry

    lax.fori_loop(0, GROUP_HEADS, settle, 0)

    def pass_corners(h):
        along(came_x, lambda side: x_side(h, side).wait_recv())
        corners(have_z, lambda column, side: corner(h, column, side).start())

    pass_corners(0)
    along(have_z, lambda side: z_side(1, side).start())
    pass_corners(1)
    along(have_z, lambda side: z_side(2, side).start())

    def out_cols(h):
        first = ((2 * core + half) * GROUP_HEADS + h) * HEAD_DIM
        return pl.ds(pl.multiple_of(first, HEAD_DIM), HEAD_DIM)

    def out_copy(pair_of, h, n):
        two = pl.ds(2 * pair_of, 2)
        return remote(
            stage.at[h, 2 * others[n][0] + others[n][1], two], out_ref.at[two, :, out_cols(h)],
            out_send_sem, out_recv_sem, pair_of, mate(others[n]),
        )

    def out_own(pair_of, h):
        two = pl.ds(2 * pair_of, 2)
        return pltpu.make_async_copy(
            stage.at[h, own_block, two], out_ref.at[two, :, out_cols(h)], out_sem.at[pair_of]
        )

    def hand_out(pair_of, h):
        for n in (1, 2, 0):
            out_copy(pair_of, h, n).start()
        out_own(pair_of, h).start()

    def bias_of(i, j):
        gone = [jnp.logical_not(have_x[i // 3])] if i in (0, 3) else []
        gone += [jnp.logical_not(have_z[j // 3])] if j in (0, 3) else []
        if not gone:
            return None
        return jnp.where(functools.reduce(jnp.logical_or, gone), NEG, 0.0).astype(F32)

    bias = {(i, j): bias_of(i, j) for i in range(4) for j in range(4)}

    def attend(h, carry):
        along(came_z, lambda side: z_side(h, side).wait_recv())
        corners(came_z, lambda column, side: corner(h, column, side).wait_recv())

        def prepare(e, inner):
            ext_t[e // 4, e % 4] = ext[h, e // 4, e % 4].astype(F32).T.astype(BF16)
            return inner

        lax.fori_loop(0, 16, prepare, 0)
        top, total, out_t, dq_t = [None] * 4, [None] * 4, [None] * 4, [None] * 4
        delta, inverse = [None] * 4, [None] * 4

        def add(held, b, n, term):
            held[b] = term if n == 0 else held[b] + term

        def scores_of(b, n):
            spot = spots_of(b)[n]
            s = dot(ext[h, spot[0], spot[1], :, :HEAD_DIM], query_t[h, b])
            score[b % 2, n] = s
            most = jnp.max(s, axis=0, keepdims=True)
            if bias[spot] is not None:
                most = most + bias[spot]
            top[b] = most if n == 0 else jnp.maximum(top[b], most)

        def forward(b, n):
            i, j = spots_of(b)[n]
            shift = top[b] * (SCALE * LOG2E)
            if bias[i, j] is not None:
                shift = shift - bias[i, j]
            p = jnp.exp2(score[b % 2, n] * (SCALE * LOG2E) - shift)
            add(total, b, n, jnp.sum(p, axis=0, keepdims=True))
            p_low = p.astype(BF16)
            prob[b, n] = p_low
            add(out_t, b, n, dot(ext_t[i, j, HEAD_DIM:, :], p_low))
            if n == 8:
                inverse[b] = 1.0 / total[b]
                full = out_t[b] * inverse[b]
                grad_f = grad_t[h, b].astype(F32)
                delta[b] = jnp.sum(grad_f * full, axis=0, keepdims=True)
                stage[h, b, 0] = full.T.astype(BF16)
                grad_s[b] = (grad_f * inverse[b]).astype(BF16)
                query_s[b] = (query_t[h, b].astype(F32) * (inverse[b] * SCALE)).astype(BF16)

        def backward(b, n):
            i, j = spots_of(b)[n]
            dp = dot(ext[h, i, j, :, HEAD_DIM:], grad_t[h, b])
            ds = (prob[b, n].astype(F32) * (dp - delta[b])).astype(BF16)
            grad_score[b, n] = ds
            add(dq_t, b, n, dot(ext_t[i, j, :HEAD_DIM, :], ds))
            if n == 8:
                stage[h, b, 1] = (dq_t[b] * (inverse[b] * SCALE)).T.astype(BF16)

        for turn in range(6):
            for n in range(9):
                for step, b in ((scores_of, turn), (forward, turn - 1), (backward, turn - 2)):
                    if 0 <= b < 4:
                        step(b, n)

        def key_terms(i, j):
            k_sum = v_sum = None
            for b in range(4):
                if (i, j) in spots_of(b):
                    n = spots_of(b).index((i, j))
                    k_term = dot_nt(grad_score[b, n], query_s[b])
                    v_term = dot_nt(prob[b, n], grad_s[b])
                    k_sum = k_term if k_sum is None else k_sum + k_term
                    v_sum = v_term if v_sum is None else v_sum + v_term
            return ((slice(0, HEAD_DIM), k_sum), (slice(HEAD_DIM, 2 * HEAD_DIM), v_sum))

        for kind in range(2):
            for side in range(2):
                for i in ((0, 3), (1, 2))[kind]:
                    for lanes, value in key_terms(i, 3 * side):
                        back_z[h, side, SEAT[i], :, lanes] = value.astype(BF16)
            along(have_z, lambda side: z_back(h, side, kind).start())
        hand_out(0, h)
        for i in (0, 3, 1, 2):
            for j in (1, 2):
                for lanes, value in key_terms(i, j):
                    keep[h, i, j - 1, :, lanes] = value
        return carry

    def turn_x(h):
        along(came_z, lambda side: z_back(h, side, 0).wait_recv())
        for side in range(2):
            for j in range(2):
                both = keep[h, 3 * side, j] + from_z[h, j, side].astype(F32)
                back_x[h, side, j] = both.astype(BF16)
        along(have_x, lambda side: x_back(h, side).start())

    def heads(h, carry):
        attend(h, 0)

        @pl.when(h == 0)
        def _():
            pass_corners(GROUP_HEADS - 1)

        @pl.when(h > 0)
        def _():
            turn_x(h - 1)

        return carry

    lax.fori_loop(0, GROUP_HEADS, heads, 0)
    turn_x(GROUP_HEADS - 1)

    def finish(h, carry):
        along(came_z, lambda side: z_back(h, side, 1).wait_recv())
        along(came_x, lambda side: x_back(h, side).wait_recv())
        for b in range(4):
            i, j = b // 2, b % 2
            whole = keep[h, 1 + i, j] + from_z[h, j, 2 + i].astype(F32)
            low = (whole + from_x[h, i, j].astype(F32)).astype(BF16)
            stage[h, b, 2] = low[:, :HEAD_DIM]
            stage[h, b, 3] = low[:, HEAD_DIM:]
        hand_out(1, h)
        return carry

    lax.fori_loop(0, GROUP_HEADS, finish, 0)

    for a in range(3):
        pair_copy(a).wait_send()
    for n in range(3):
        grad_copy(n).wait_send()

    def sent(h, carry):
        many = pl.ds(0, 16 * (chips - 1))
        pltpu.make_async_copy(recv.at[h, many], recv.at[h, many], all_send_sem.at[h]).wait()
        along(have_x, lambda side: x_side(h, side).wait_send())
        along(have_z, lambda side: z_side(h, side).wait_send())
        corners(have_z, lambda column, side: corner(h, column, side).wait_send())
        for kind in range(2):
            along(have_z, lambda side: z_back(h, side, kind).wait_send())
        along(have_x, lambda side: x_back(h, side).wait_send())
        return carry

    lax.fori_loop(0, GROUP_HEADS, sent, 0)
    for pair_of in range(2):
        two = pl.ds(2 * pair_of, 2)
        mine = out_ref.at[two, :, pl.ds(0, width)]
        far = out_ref.at[two, :, pl.ds(0, 3 * width)]
        pltpu.make_async_copy(mine, mine, out_sem.at[pair_of]).wait()
        pltpu.make_async_copy(far, far, out_send_sem.at[pair_of]).wait()
        pltpu.make_async_copy(far, far, out_recv_sem.at[pair_of]).wait()


def deal(in_ref, *refs):
    outs, (held, in_sem, out_sem) = refs[:4], refs[4:]
    into = [pltpu.make_async_copy(in_ref.at[n], held.at[n], in_sem.at[n]) for n in range(4)]
    onward = [pltpu.make_async_copy(held.at[n], outs[n], out_sem.at[n]) for n in range(4)]
    for copy in into:
        copy.start()
    for n in range(4):
        into[n].wait()
        onward[n].start()
    for copy in onward:
        copy.wait()


def shards(nt, nh, query_seq, key_seq, value_seq, tile_order, grad_output):
    block_shape = grad_output.shape
    cols = block_shape[2]
    tok, channels = query_seq.shape
    low = jax.ShapeDtypeStruct((tok, channels), BF16)
    hbm = pl.BlockSpec(memory_space=pl.ANY)
    vmem = pl.BlockSpec(memory_space=pltpu.VMEM)
    gh, d = GROUP_HEADS, HEAD_DIM
    dma = pltpu.SemaphoreType.DMA
    whole = pl.pallas_call(
        functools.partial(kernel, nt, nh, cols),
        out_shape=jax.ShapeDtypeStruct((4, tok, channels), BF16),
        in_specs=[hbm, hbm, hbm, vmem, hbm],
        out_specs=hbm,
        scratch_shapes=[
            pltpu.VMEM((3, 2 * tok, 2 * gh * d), BF16),
            pltpu.VMEM((2 * tok, 2 * tok), BF16),
            pltpu.VMEM((gh, 2, 2 * tok, 3 * d), BF16),
            pltpu.VMEM((gh, 4 * tok, 3 * d), BF16),
            pltpu.VMEM((4, tok, 4 * tok), BF16),
            pltpu.VMEM((gh, 4, 4, tok, 2 * d), BF16),
            pltpu.VMEM((4, 4, 2 * d, tok), BF16),
            pltpu.VMEM((gh, 4, d, tok), BF16),
            pltpu.VMEM((4, tok, gh * d), BF16),
            pltpu.VMEM((gh, 4, d, tok), BF16),
            pltpu.VMEM((2, 9, tok, tok), F32),
            pltpu.VMEM((4, 9, tok, tok), BF16),
            pltpu.VMEM((4, 9, tok, tok), BF16),
            pltpu.VMEM((4, d, tok), BF16),
            pltpu.VMEM((4, d, tok), BF16),
            pltpu.VMEM((gh, 4, 2, tok, 2 * d), F32),
            pltpu.VMEM((gh, 2, 4, tok, 2 * d), BF16),
            pltpu.VMEM((gh, 2, 4, tok, 2 * d), BF16),
            pltpu.VMEM((gh, 2, 2, tok, 2 * d), BF16),
            pltpu.VMEM((gh, 2, 2, tok, 2 * d), BF16),
            pltpu.VMEM((gh, 4, 4, tok, d), BF16),
            dma((3,)), dma((3,)), dma((3,)),
            dma, dma((3,)), dma((3,)),
            dma((gh,)), dma((gh,)), dma((gh,)),
            dma((gh, 4)), dma((gh, 4)), dma((gh, 4)), dma((gh, 4)),
            dma((gh, 4)), dma((gh, 4)), dma((gh, 2)), dma((gh, 2)),
            dma((2,)), dma((2,)), dma((2,)),
        ],
        compiler_params=pltpu.CompilerParams(
            collective_id=0, has_side_effects=True, vmem_limit_bytes=60 * 2**20
        ),
        cost_estimate=pl.CostEstimate(
            flops=12 * 4 * gh * 9 * tok * tok * d,
            bytes_accessed=16 * tok * channels,
            transcendentals=4 * gh * 9 * tok * tok,
        ),
    )(query_seq, key_seq, value_seq, tile_order.reshape(nt * nh, tok), grad_output.reshape(tok, channels))
    outs = pl.pallas_call(
        deal,
        out_shape=[low] * 4,
        in_specs=[hbm],
        out_specs=[hbm] * 4,
        scratch_shapes=[pltpu.VMEM((4, tok, channels), BF16), dma((4,)), dma((4,))],
        compiler_params=pltpu.CompilerParams(vmem_limit_bytes=60 * 2**20),
    )(whole)
    return tuple(o.reshape(block_shape) for o in outs)


def solution(mesh):
    seq = P(("ta", "ha"), None)
    grid = P("ta", "ha", None, None)
    return jax.shard_map(
        functools.partial(shards, mesh.shape["ta"], mesh.shape["ha"]),
        mesh=mesh,
        in_specs=(seq, seq, seq, P(), grid),
        out_specs=(grid,) * 4,
        check_vma=False,
    )
```

```python
import functools

import jax
import jax.numpy as jnp
from jax import lax
from jax.experimental import pallas as pl
from jax.experimental.pallas import tpu as pltpu
from jax.sharding import PartitionSpec as P

HEADS = 12
HEAD_DIM = 128
GROUP_HEADS = 3
TILE_FRAMES = 4
TILE_ROWS = 8
SCALE = HEAD_DIM ** (-0.5)
LOG2E = 1.4426950408889634
NEG = -1e30
MESH = pl.DeviceIdType.MESH
F32 = jnp.float32
BF16 = jnp.bfloat16
SEAT = {0: 0, 3: 1, 1: 2, 2: 3}


def dot(a, b):
    return jnp.dot(a, b, preferred_element_type=F32)


def dot_nt(a, b):
    return lax.dot_general(a, b, (((1,), (1,)), ((), ())), preferred_element_type=F32)


def iota(shape, dim):
    return lax.broadcasted_iota(jnp.int32, shape, dim)


def spots_of(b):
    return [(b // 2 + di, b % 2 + dj) for di in range(3) for dj in range(3)]


def kernel(
    nt, nh, cols,
    q_ref, k_ref, v_ref, order_ref, grad_ref,
    out_ref,
    pair, sort_one, send, recv, place, ext, ext_t, query_t, grad_blocks, grad_t,
    score, prob, grad_score, query_s, grad_s, keep, keep_z,
    back_z, from_z, back_x, from_x, back_cross, from_cross, stage,
    pair_sem, pair_send_sem, pair_recv_sem,
    grad_sem, grad_send_sem, grad_recv_sem,
    all_sem, all_send_sem, all_recv_sem,
    side_send_sem, side_recv_sem, corner_send_sem, corner_recv_sem, cross_send_sem,
    back_z_send_sem, back_z_recv_sem, back_x_send_sem, back_x_recv_sem,
    back_cross_send_sem, back_cross_recv_sem,
    out_sem, out_send_sem, out_recv_sem,
):
    tok = TILE_FRAMES * TILE_ROWS * cols
    nk, nz = nt // 2, nh // 2
    chips = nk * nh
    width = GROUP_HEADS * HEAD_DIM
    ta, ha = lax.axis_index("ta"), lax.axis_index("ha")
    kk, core = ta // 2, ta % 2
    zz, half = ha // 2, ha % 2
    chip = kk * nh + ha
    others = [(1 - core, half), (core, 1 - half), (1 - core, 1 - half)]

    def mate(where):
        return (2 * kk + where[0], 2 * zz + where[1])

    have_x = (kk > 0, kk < nk - 1)
    have_z = (zz > 0, zz < nz - 1)
    far_x = (kk == nk // 2, kk == nk // 2 - 1)
    half_tok = tok // 2
    part_rows = (pl.ds(0, half_tok), pl.ds(half_tok, half_tok))

    nothing = jnp.zeros((tok, 2 * HEAD_DIM), BF16)
    for side in range(2):

        @pl.when(jnp.logical_not(have_x[side]))
        def _(side=side):
            def clear(h, carry):
                for n in range(4):
                    ext[h, 3 * side, n] = nothing
                for n in range(2):
                    from_x[h, side, n] = nothing
                return carry

            lax.fori_loop(0, GROUP_HEADS, clear, 0)

        @pl.when(jnp.logical_not(have_x[side]) | far_x[side])
        def _(side=side):
            def clear(h, carry):
                for n in range(2):
                    from_cross[h, side, n] = jnp.zeros((half_tok, 2 * HEAD_DIM), BF16)
                return carry

            lax.fori_loop(0, GROUP_HEADS, clear, 0)

        @pl.when(jnp.logical_not(have_z[side]))
        def _(side=side):
            def clear(h, carry):
                for n in range(4):
                    ext[h, n, 3 * side] = nothing
                    from_z[h, side, n] = nothing
                return carry

            lax.fori_loop(0, GROUP_HEADS, clear, 0)

    barrier = pltpu.get_barrier_semaphore()

    def greet(d, carry):
        to = lax.rem(chip + d, chips)
        pl.semaphore_signal(
            barrier, inc=1, device_id=(2 * (to // nh) + core, to % nh), device_id_type=MESH
        )
        return carry

    lax.fori_loop(1, chips, greet, 0)
    for where in ((1 - core, half), (1 - core, 1 - half)):
        pl.semaphore_signal(barrier, inc=1, device_id=mate(where), device_id_type=MESH)

    seq = (q_ref, k_ref, v_ref)
    own_rows = pl.ds(pl.multiple_of(core * tok, tok), tok)

    def head_cols(h, n, of):
        inner = (n % 2) * width + h * HEAD_DIM
        return pl.ds(pl.multiple_of(of * 2 * width + inner, HEAD_DIM), HEAD_DIM)

    def pair_own(h, n):
        return pltpu.make_async_copy(
            seq[n // 2].at[:, head_cols(h, n, core)],
            pair.at[n // 2, own_rows, head_cols(h, n, 0)],
            pair_sem.at[h, n],
        )

    def start_own(h, carry):
        for n in range(6):
            pair_own(h, n).start()
        return carry

    lax.fori_loop(0, GROUP_HEADS, start_own, 0)

    def group_cols(where, n=width):
        return pl.ds(pl.multiple_of((2 * where[0] + where[1]) * width, width), width)

    own_block = 2 * core + half
    pltpu.make_async_copy(
        grad_ref.at[:, group_cols((core, half))], grad_blocks.at[own_block], grad_sem
    ).start()

    pl.semaphore_wait(barrier, chips + 1)

    def pair_copy(h, n):
        return pltpu.make_async_remote_copy(
            src_ref=seq[n // 2].at[:, head_cols(h, n, 1 - core)],
            dst_ref=pair.at[n // 2, own_rows, head_cols(h, n, 0)],
            send_sem=pair_send_sem.at[h, n],
            recv_sem=pair_recv_sem.at[h, n],
            device_id=mate((1 - core, half)),
            device_id_type=MESH,
        )

    def grad_copy(n):
        return pltpu.make_async_remote_copy(
            src_ref=grad_ref.at[:, group_cols(others[n])],
            dst_ref=grad_blocks.at[own_block],
            send_sem=grad_send_sem.at[n],
            recv_sem=grad_recv_sem.at[n],
            device_id=mate(others[n]),
            device_id_type=MESH,
        )

    def start_pair(h, carry):
        for n in range(6):
            pair_copy(h, n).start()
        return carry

    lax.fori_loop(0, GROUP_HEADS, start_pair, 0)
    for n in range(3):
        grad_copy(n).start()

    def decode(t):
        frame = t // (nh * TILE_ROWS * cols)
        row = (t // cols) % (nh * TILE_ROWS)
        frame_block, row_block = frame // TILE_FRAMES, row // TILE_ROWS
        inside = ((frame % TILE_FRAMES) * TILE_ROWS + row % TILE_ROWS) * cols + t % cols
        return frame_block, row_block, inside

    order = order_ref[...]
    order_t = order.T
    for cc in range(2):
        source = kk * 2 * nh + cc * nh + ha
        line = order_ref[pl.ds(source, 1), :]
        column = jnp.sum(
            jnp.where(iota(order_t.shape, 1) == source, order_t, 0), axis=1, keepdims=True
        )
        line_f, line_r, _ = decode(line)
        col_f, col_r, _ = decode(column)
        same = (line_f * nh + line_r) == (col_f * nh + col_r)
        earlier = iota((tok, tok), 0) < iota((tok, tok), 1)
        second = jnp.sum(jnp.where(same & earlier, 1, 0), axis=0, keepdims=True)
        region = (line_f // 2) * nz + line_r // 2
        seat = region * 16 + ((line_f % 2) * 2 + line_r % 2) * 4 + cc * 2 + second
        sort_one[:, cc * tok : (cc + 1) * tok] = jnp.where(
            iota((2 * tok, tok), 0) == seat, 1.0, 0.0
        ).astype(BF16)

    def all_copy(h, d):
        to = lax.rem(chip + d, chips)
        to_k, to_h = to // nh, to % nh
        region = to_k * nz + to_h // 2
        return pltpu.make_async_remote_copy(
            src_ref=send.at[h, to_h % 2, pl.ds(pl.multiple_of(region * 16, 16), 16)],
            dst_ref=recv.at[h, pl.ds(pl.multiple_of(chip * 16, 16), 16)],
            send_sem=all_send_sem.at[h],
            recv_sem=all_recv_sem.at[h],
            device_id=(2 * to_k + core, to_h),
            device_id_type=MESH,
        )

    def all_own(h):
        region = kk * nz + zz
        return pltpu.make_async_copy(
            send.at[h, half, pl.ds(pl.multiple_of(region * 16, 16), 16)],
            recv.at[h, pl.ds(pl.multiple_of(chip * 16, 16), 16)],
            all_sem.at[h],
        )

    def send_head(h, carry):
        for n in range(6):
            pair_own(h, n).wait()
            pair_copy(h, n).wait_recv()
        for a in range(3):
            left = pl.ds(pl.multiple_of(h * HEAD_DIM, HEAD_DIM), HEAD_DIM)
            right = pl.ds(pl.multiple_of(width + h * HEAD_DIM, HEAD_DIM), HEAD_DIM)
            both = jnp.concatenate([pair[a, :, left], pair[a, :, right]], axis=1)
            sorted_rows = dot(sort_one[...], both).astype(BF16)
            into = slice(a * HEAD_DIM, (a + 1) * HEAD_DIM)
            send[h, 0, :, into] = sorted_rows[:, :HEAD_DIM]
            send[h, 1, :, into] = sorted_rows[:, HEAD_DIM:]
        all_own(h).start()

        def push(d, inner):
            all_copy(h, d).start()
            return inner

        lax.fori_loop(1, chips, push, 0)
        return carry

    lax.fori_loop(0, GROUP_HEADS, send_head, 0)

    frame_block, row_block, inside = decode(order_t)
    block_of = frame_block * nh + row_block
    code = iota(order_t.shape, 0) * tok + inside
    found = []
    for b in range(4):
        mine = block_of == (2 * kk + b // 2) * nh + 2 * zz + b % 2
        found.append(jnp.min(jnp.where(mine, code, tok * tok), axis=0, keepdims=True) % tok)
        found.append(jnp.max(jnp.where(mine, code, 0), axis=0, keepdims=True) % tok)
    table = jnp.concatenate(found, axis=0).astype(F32).astype(BF16)
    rows = 4 * tok
    number = iota((nt * nh, rows), 1)
    from_chip, place_in = number // 16, number % 16
    sender = (from_chip // nh) * 2 * nh + ((place_in // 2) % 2) * nh + from_chip % nh
    spread = jnp.where(iota((nt * nh, rows), 0) == sender, 1.0, 0.0).astype(BF16)
    wide = dot(table, spread)
    lane = iota((8, rows), 1) % 16
    chosen = iota((8, rows), 0) == (lane // 4) * 2 + lane % 2
    position = jnp.sum(jnp.where(chosen, wide, 0.0), axis=0, keepdims=True).astype(jnp.int32)
    position = position + (iota((1, rows), 1) % 16 // 4) * tok

    def fill_place(b, carry):
        place[b] = jnp.where(iota((tok, rows), 0) + b * tok == position, 1.0, 0.0).astype(BF16)
        return carry

    lax.fori_loop(0, 4, fill_place, 0)

    pltpu.make_async_copy(
        grad_ref.at[:, group_cols((core, half))], grad_blocks.at[own_block], grad_sem
    ).wait()
    for n in range(3):
        grad_copy(n).wait_recv()

    def turn_grad(b, carry):
        for h in range(GROUP_HEADS):
            piece = grad_blocks[b, :, h * HEAD_DIM : (h + 1) * HEAD_DIM]
            grad_t[h, b] = piece.astype(F32).T.astype(BF16)
        return carry

    lax.fori_loop(0, 4, turn_grad, 0)

    def x_device(side):
        return (ta + 2 * (2 * side - 1), ha)

    def z_device(side):
        return (ta, ha + 2 * (2 * side - 1))

    def remote(src, dst, sends, recvs, index, device):
        return pltpu.make_async_remote_copy(
            src_ref=src, dst_ref=dst, send_sem=sends.at[index], recv_sem=recvs.at[index],
            device_id=device, device_id_type=MESH,
        )

    def x_side(h, side):
        return remote(
            ext.at[h, 1 + side, pl.ds(1, 2)], ext.at[h, 3 - 3 * side, pl.ds(1, 2)],
            side_send_sem, side_recv_sem, (h, side), x_device(side),
        )

    def z_side(h, side):
        return remote(
            ext.at[h, pl.ds(1, 2), 1 + side], ext.at[h, pl.ds(1, 2), 3 - 3 * side],
            side_send_sem, side_recv_sem, (h, 2 + side), z_device(side),
        )

    def corner(h, column, side, part):
        return remote(
            ext.at[h, 3 * column, 1 + side, part_rows[part]],
            ext.at[h, 3 * column, 3 - 3 * side, part_rows[part]],
            corner_send_sem, corner_recv_sem, (h, 4 * part + 2 * column + side), z_device(side),
        )

    def cross(h, column, side):
        return pltpu.make_async_remote_copy(
            src_ref=ext.at[h, 1 + column, 3 * side, part_rows[1]],
            dst_ref=ext.at[h, 3 - 3 * column, 3 * side, part_rows[1]],
            send_sem=cross_send_sem.at[h, 2 * column + side],
            recv_sem=corner_recv_sem.at[h, 4 + 2 * (1 - column) + 1 - side],
            device_id=x_device(column),
            device_id_type=MESH,
        )

    def z_back(h, side, kind, part):
        two = pl.ds(2 * kind, 2)
        return remote(
            back_z.at[h, side, two, part_rows[part]], from_z.at[h, 1 - side, two, part_rows[part]],
            back_z_send_sem, back_z_recv_sem, (h, 2 * (kind + part) + side), z_device(side),
        )

    def z_back_far(h, column, side):
        return remote(
            back_z.at[h, side, column, part_rows[1]], from_z.at[h, 1 - side, column, part_rows[1]],
            back_z_send_sem, back_z_recv_sem, (h, 6 + 2 * column + side), z_device(side),
        )

    def x_back(h, side, part):
        both = pl.ds(0, 2)
        return remote(
            back_x.at[h, side, both, part_rows[part]], from_x.at[h, 1 - side, both, part_rows[part]],
            back_x_send_sem, back_x_recv_sem, (h, 2 * part + side), x_device(side),
        )

    def x_cross(h, column, side):
        return remote(
            back_cross.at[h, column, side], from_cross.at[h, 1 - column, side],
            back_cross_send_sem, back_cross_recv_sem, (h, 2 * column + side), x_device(column),
        )

    def along(have, step):
        for side in range(2):
            pl.when(have[side])(functools.partial(step, side))

    def corners(have, step, only=None):
        for column in range(2):
            for side in range(2):
                when = have_x[column] & have[side]
                if only is not None:
                    when = when & only[column]
                pl.when(when)(functools.partial(step, column, side))

    near_x = tuple(jnp.logical_not(f) for f in far_x)
    came_x, came_z = have_x[::-1], have_z[::-1]
    at_near = tuple(have_x[n] & near_x[n] for n in range(2))
    at_far = tuple(have_x[n] & far_x[n] for n in range(2))

    def gather_in(h, carry):
        all_own(h).wait()
        many = pl.ds(0, 16 * (chips - 1))
        pltpu.make_async_copy(recv.at[h, many], recv.at[h, many], all_recv_sem.at[h]).wait()
        return carry

    lax.fori_loop(0, GROUP_HEADS, gather_in, 0)

    def start_sides(h):
        along(have_x, lambda side: x_side(h, side).start())
        along(have_z, lambda side: z_side(h, side).start())

    def settle(h, carry):
        def one_block(b, inner):
            grid_rows = dot(place[b], recv[h])
            query_t[h, b] = grid_rows[:, :HEAD_DIM].T.astype(BF16)
            ext[h, 1 + b // 2, 1 + b % 2] = grid_rows[:, HEAD_DIM:].astype(BF16)
            return inner

        lax.fori_loop(0, 4, one_block, 0)
        pl.when(h == 0)(lambda: start_sides(0))
        return carry

    lax.fori_loop(0, GROUP_HEADS, settle, 0)

    def pass_corners(h):
        along(came_x, lambda side: x_side(h, side).wait_recv())
        corners(have_z, lambda column, side: corner(h, column, side, 0).start())
        corners(have_z, lambda column, side: corner(h, column, side, 1).start(), far_x)
        along(came_z, lambda side: z_side(h, side).wait_recv())
        corners(have_z, lambda column, side: cross(h, column, side).start(), near_x)

    pass_corners(0)
    start_sides(1)
    start_sides(2)

    def out_cols(h):
        first = ((2 * core + half) * GROUP_HEADS + h) * HEAD_DIM
        return pl.ds(pl.multiple_of(first, HEAD_DIM), HEAD_DIM)

    def out_copy(pair_of, h, n):
        two = pl.ds(2 * pair_of, 2)
        return remote(
            stage.at[h, 2 * others[n][0] + others[n][1], two], out_ref.at[two, :, out_cols(h)],
            out_send_sem, out_recv_sem, pair_of, mate(others[n]),
        )

    def out_own(pair_of, h):
        two = pl.ds(2 * pair_of, 2)
        return pltpu.make_async_copy(
            stage.at[h, own_block, two], out_ref.at[two, :, out_cols(h)], out_sem.at[pair_of]
        )

    def hand_out(pair_of, h):
        for n in (1, 2, 0):
            out_copy(pair_of, h, n).start()
        out_own(pair_of, h).start()

    def bias_of(i, j):
        gone = [jnp.logical_not(have_x[i // 3])] if i in (0, 3) else []
        gone += [jnp.logical_not(have_z[j // 3])] if j in (0, 3) else []
        if not gone:
            return None
        return jnp.where(functools.reduce(jnp.logical_or, gone), NEG, 0.0).astype(F32)

    bias = {(i, j): bias_of(i, j) for i in range(4) for j in range(4)}

    def turn(h):
        first, later = slice(0, half_tok), slice(half_tok, tok)
        along(came_z, lambda side: z_back(h, side, 0, 0).wait_recv())
        for column in range(2):
            for j in range(2):
                both = keep[h, 3 * column, j, first] + from_z[h, j, column, first].astype(F32)
                back_x[h, column, j, first] = both.astype(BF16)
        along(have_x, lambda side: x_back(h, side, 0).start())
        corners(came_z, lambda column, side: z_back_far(h, column, side).wait_recv(), far_x)

        def add_far(column):
            for j in range(2):
                both = keep[h, 3 * column, j, later] + from_z[h, j, column, later].astype(F32)
                back_x[h, column, j, later] = both.astype(BF16)
            x_back(h, column, 1).start()

        along(at_far, add_far)
        for column in range(2):
            for side in range(2):
                pl.when(at_near[1 - column] & have_z[side])(
                    functools.partial(lambda c, d: x_cross(h, c, d).wait_recv(), column, side)
                )
        for side in range(2):
            for i in range(2):
                both = keep_z[h, side, i] + from_cross[h, i, side].astype(F32)
                back_z[h, side, 2 + i, later] = both.astype(BF16)
        along(have_z, lambda side: z_back(h, side, 1, 1).start())

    def finish(h):
        for part in range(2):
            along(came_z, lambda side: z_back(h, side, 1, part).wait_recv())
            along(came_x, lambda side: x_back(h, side, part).wait_recv())
        for b in range(4):
            i, j = b // 2, b % 2
            whole = keep[h, 1 + i, j] + from_z[h, j, 2 + i].astype(F32)
            low = (whole + from_x[h, i, j].astype(F32)).astype(BF16)
            stage[h, b, 2] = low[:, :HEAD_DIM]
            stage[h, b, 3] = low[:, HEAD_DIM:]
        hand_out(1, h)

    def attend(h, carry):
        for part in range(2):
            corners(came_z, lambda column, side: corner(h, column, side, part).wait_recv())

        def prepare(e, inner):
            ext_t[e // 4, e % 4] = ext[h, e // 4, e % 4].astype(F32).T.astype(BF16)
            return inner

        lax.fori_loop(0, 16, prepare, 0)
        top, total, out_t, dq_t = [None] * 4, [None] * 4, [None] * 4, [None] * 4
        delta, inverse = [None] * 4, [None] * 4

        def add(held, b, n, term):
            held[b] = term if n == 0 else held[b] + term

        def scores_of(b, n):
            spot = spots_of(b)[n]
            s = dot(ext[h, spot[0], spot[1], :, :HEAD_DIM], query_t[h, b])
            score[b % 2, n] = s
            most = jnp.max(s, axis=0, keepdims=True)
            if bias[spot] is not None:
                most = most + bias[spot]
            top[b] = most if n == 0 else jnp.maximum(top[b], most)

        def forward(b, n):
            i, j = spots_of(b)[n]
            shift = top[b] * (SCALE * LOG2E)
            if bias[i, j] is not None:
                shift = shift - bias[i, j]
            p = jnp.exp2(score[b % 2, n] * (SCALE * LOG2E) - shift)
            add(total, b, n, jnp.sum(p, axis=0, keepdims=True))
            p_low = p.astype(BF16)
            prob[b, n] = p_low
            add(out_t, b, n, dot(ext_t[i, j, HEAD_DIM:, :], p_low))
            if n == 8:
                inverse[b] = 1.0 / total[b]
                full = out_t[b] * inverse[b]
                grad_f = grad_t[h, b].astype(F32)
                delta[b] = jnp.sum(grad_f * full, axis=0, keepdims=True)
                stage[h, b, 0] = full.T.astype(BF16)
                grad_s[b] = (grad_f * inverse[b]).astype(BF16)
                query_s[b] = (query_t[h, b].astype(F32) * (inverse[b] * SCALE)).astype(BF16)

        def backward(b, n):
            i, j = spots_of(b)[n]
            dp = dot(ext[h, i, j, :, HEAD_DIM:], grad_t[h, b])
            ds = (prob[b, n].astype(F32) * (dp - delta[b])).astype(BF16)
            grad_score[b, n] = ds
            add(dq_t, b, n, dot(ext_t[i, j, :HEAD_DIM, :], ds))
            if n == 8:
                stage[h, b, 1] = (dq_t[b] * (inverse[b] * SCALE)).T.astype(BF16)

        for beat in range(6):
            for n in range(9):
                for step, b in ((scores_of, beat), (forward, beat - 1), (backward, beat - 2)):
                    if 0 <= b < 4:
                        step(b, n)

        hand_out(0, h)

        pl.when(h == 0)(lambda: pass_corners(1))
        pl.when(h > 0)(lambda: turn(h - 1))

        def key_terms(i, j):
            k_sum = v_sum = None
            for b in range(4):
                if (i, j) in spots_of(b):
                    n = spots_of(b).index((i, j))
                    k_term = dot_nt(grad_score[b, n], query_s[b])
                    v_term = dot_nt(prob[b, n], grad_s[b])
                    k_sum = k_term if k_sum is None else k_sum + k_term
                    v_sum = v_term if v_sum is None else v_sum + v_term
            return ((slice(0, HEAD_DIM), k_sum), (slice(HEAD_DIM, 2 * HEAD_DIM), v_sum))

        first, later = slice(0, half_tok), slice(half_tok, tok)
        for side in range(2):
            for column in range(2):
                for lanes, value in key_terms(3 * column, 3 * side):
                    low = value.astype(BF16)
                    back_z[h, side, column, :, lanes] = low
                    back_cross[h, column, side, :, lanes] = low[later]
        along(have_z, lambda side: z_back(h, side, 0, 0).start())
        corners(have_z, lambda column, side: z_back_far(h, column, side).start(), far_x)
        corners(have_z, lambda column, side: x_cross(h, column, side).start(), near_x)
        for column in range(2):
            for j in (1, 2):
                for lanes, value in key_terms(3 * column, j):
                    keep[h, 3 * column, j - 1, :, lanes] = value
                    back_x[h, column, j - 1, later, lanes] = value[later].astype(BF16)
        along(at_near, lambda side: x_back(h, side, 1).start())
        for side in range(2):
            for i in (1, 2):
                for lanes, value in key_terms(i, 3 * side):
                    back_z[h, side, SEAT[i], first, lanes] = value[first].astype(BF16)
                    keep_z[h, side, i - 1, :, lanes] = value[later]
        along(have_z, lambda side: z_back(h, side, 1, 0).start())
        for i in (1, 2):
            for j in (1, 2):
                for lanes, value in key_terms(i, j):
                    keep[h, i, j - 1, :, lanes] = value
        pl.when(h == 0)(lambda: pass_corners(2))
        pl.when(h > 0)(lambda: finish(h - 1))
        return carry

    lax.fori_loop(0, GROUP_HEADS, attend, 0)
    turn(GROUP_HEADS - 1)
    finish(GROUP_HEADS - 1)

    for n in range(3):
        grad_copy(n).wait_send()

    def sent(h, carry):
        for n in range(6):
            pair_copy(h, n).wait_send()
        many = pl.ds(0, 16 * (chips - 1))
        pltpu.make_async_copy(recv.at[h, many], recv.at[h, many], all_send_sem.at[h]).wait()
        along(have_x, lambda side: x_side(h, side).wait_send())
        along(have_z, lambda side: z_side(h, side).wait_send())
        corners(have_z, lambda column, side: corner(h, column, side, 0).wait_send())
        corners(have_z, lambda column, side: corner(h, column, side, 1).wait_send(), far_x)
        corners(have_z, lambda column, side: cross(h, column, side).wait_send(), near_x)
        for kind, part in ((0, 0), (1, 0), (1, 1)):
            along(have_z, lambda side: z_back(h, side, kind, part).wait_send())
        corners(have_z, lambda column, side: z_back_far(h, column, side).wait_send(), far_x)
        corners(have_z, lambda column, side: x_cross(h, column, side).wait_send(), near_x)
        for part in range(2):
            along(have_x, lambda side: x_back(h, side, part).wait_send())
        return carry

    lax.fori_loop(0, GROUP_HEADS, sent, 0)
    for pair_of in range(2):
        two = pl.ds(2 * pair_of, 2)
        mine = out_ref.at[two, :, pl.ds(0, width)]
        far = out_ref.at[two, :, pl.ds(0, 3 * width)]
        pltpu.make_async_copy(mine, mine, out_sem.at[pair_of]).wait()
        pltpu.make_async_copy(far, far, out_send_sem.at[pair_of]).wait()
        pltpu.make_async_copy(far, far, out_recv_sem.at[pair_of]).wait()


def deal(in_ref, *refs):
    outs, (held, in_sem, out_sem) = refs[:4], refs[4:]
    into = [pltpu.make_async_copy(in_ref.at[n], held.at[n], in_sem.at[n]) for n in range(4)]
    onward = [pltpu.make_async_copy(held.at[n], outs[n], out_sem.at[n]) for n in range(4)]
    for copy in into:
        copy.start()
    for n in range(4):
        into[n].wait()
        onward[n].start()
    for copy in onward:
        copy.wait()


def shards(nt, nh, query_seq, key_seq, value_seq, tile_order, grad_output):
    block_shape = grad_output.shape
    cols = block_shape[2]
    tok, channels = query_seq.shape
    low = jax.ShapeDtypeStruct((tok, channels), BF16)
    hbm = pl.BlockSpec(memory_space=pl.ANY)
    vmem = pl.BlockSpec(memory_space=pltpu.VMEM)
    gh, d = GROUP_HEADS, HEAD_DIM
    dma = pltpu.SemaphoreType.DMA
    whole = pl.pallas_call(
        functools.partial(kernel, nt, nh, cols),
        out_shape=jax.ShapeDtypeStruct((4, tok, channels), BF16),
        in_specs=[hbm, hbm, hbm, vmem, hbm],
        out_specs=hbm,
        scratch_shapes=[
            pltpu.VMEM((3, 2 * tok, 2 * gh * d), BF16),
            pltpu.VMEM((2 * tok, 2 * tok), BF16),
            pltpu.VMEM((gh, 2, 2 * tok, 3 * d), BF16),
            pltpu.VMEM((gh, 4 * tok, 3 * d), BF16),
            pltpu.VMEM((4, tok, 4 * tok), BF16),
            pltpu.VMEM((gh, 4, 4, tok, 2 * d), BF16),
            pltpu.VMEM((4, 4, 2 * d, tok), BF16),
            pltpu.VMEM((gh, 4, d, tok), BF16),
            pltpu.VMEM((4, tok, gh * d), BF16),
            pltpu.VMEM((gh, 4, d, tok), BF16),
            pltpu.VMEM((2, 9, tok, tok), F32),
            pltpu.VMEM((4, 9, tok, tok), BF16),
            pltpu.VMEM((4, 9, tok, tok), BF16),
            pltpu.VMEM((4, d, tok), BF16),
            pltpu.VMEM((4, d, tok), BF16),
            pltpu.VMEM((gh, 4, 2, tok, 2 * d), F32),
            pltpu.VMEM((gh, 2, 2, tok // 2, 2 * d), F32),
            pltpu.VMEM((gh, 2, 4, tok, 2 * d), BF16),
            pltpu.VMEM((gh, 2, 4, tok, 2 * d), BF16),
            pltpu.VMEM((gh, 2, 2, tok, 2 * d), BF16),
            pltpu.VMEM((gh, 2, 2, tok, 2 * d), BF16),
            pltpu.VMEM((gh, 2, 2, tok // 2, 2 * d), BF16),
            pltpu.VMEM((gh, 2, 2, tok // 2, 2 * d), BF16),
            pltpu.VMEM((gh, 4, 4, tok, d), BF16),
            dma((gh, 6)), dma((gh, 6)), dma((gh, 6)),
            dma, dma((3,)), dma((3,)),
            dma((gh,)), dma((gh,)), dma((gh,)),
            dma((gh, 4)), dma((gh, 4)), dma((gh, 8)), dma((gh, 8)), dma((gh, 4)),
            dma((gh, 10)), dma((gh, 10)), dma((gh, 4)), dma((gh, 4)), dma((gh, 4)), dma((gh, 4)),
            dma((2,)), dma((2,)), dma((2,)),
        ],
        compiler_params=pltpu.CompilerParams(
            collective_id=0, has_side_effects=True, vmem_limit_bytes=60 * 2**20
        ),
        cost_estimate=pl.CostEstimate(
            flops=12 * 4 * gh * 9 * tok * tok * d,
            bytes_accessed=16 * tok * channels,
            transcendentals=4 * gh * 9 * tok * tok,
        ),
    )(query_seq, key_seq, value_seq, tile_order.reshape(nt * nh, tok), grad_output.reshape(tok, channels))
    outs = pl.pallas_call(
        deal,
        out_shape=[low] * 4,
        in_specs=[hbm],
        out_specs=[hbm] * 4,
        scratch_shapes=[pltpu.VMEM((4, tok, channels), BF16), dma((4,)), dma((4,))],
        compiler_params=pltpu.CompilerParams(vmem_limit_bytes=60 * 2**20),
    )(whole)
    return tuple(o.reshape(block_shape) for o in outs)


def solution(mesh):
    seq = P(("ta", "ha"), None)
    grid = P("ta", "ha", None, None)
    return jax.shard_map(
        functools.partial(shards, mesh.shape["ta"], mesh.shape["ha"]),
        mesh=mesh,
        in_specs=(seq, seq, seq, P(), grid),
        out_specs=(grid,) * 4,
        check_vma=False,
    )
```

```python
import functools

import jax
import jax.numpy as jnp
from jax import lax
from jax.experimental import pallas as pl
from jax.experimental.pallas import tpu as pltpu
from jax.sharding import PartitionSpec as P

HEADS = 12
HEAD_DIM = 128
GROUP_HEADS = 3
TILE_FRAMES = 4
TILE_ROWS = 8
SCALE = HEAD_DIM ** (-0.5)
LOG2E = 1.4426950408889634
NEG = -1e30
MESH = pl.DeviceIdType.MESH
F32 = jnp.float32
BF16 = jnp.bfloat16
SEAT = {0: 0, 3: 1, 1: 2, 2: 3}


def dot(a, b):
    return jnp.dot(a, b, preferred_element_type=F32)


def dot_nt(a, b):
    return lax.dot_general(a, b, (((1,), (1,)), ((), ())), preferred_element_type=F32)


def iota(shape, dim):
    return lax.broadcasted_iota(jnp.int32, shape, dim)


def spots_of(b):
    return [(b // 2 + di, b % 2 + dj) for di in range(3) for dj in range(3)]


def kernel(
    nt, nh, cols,
    q_ref, k_ref, v_ref, order_ref, grad_ref,
    out_ref,
    pair, sort_one, send, recv, place, ext, ext_t, query_t, grad_blocks, grad_t,
    score, prob, grad_score, query_s, grad_s, keep, keep_z,
    back_z, from_z, back_x, from_x, back_cross, from_cross, stage,
    pair_sem, pair_send_sem, pair_recv_sem,
    grad_sem, grad_send_sem, grad_recv_sem,
    all_sem, all_send_sem, all_recv_sem,
    side_send_sem, side_recv_sem, corner_send_sem, corner_recv_sem, cross_send_sem,
    back_z_send_sem, back_z_recv_sem, back_x_send_sem, back_x_recv_sem,
    back_cross_send_sem, back_cross_recv_sem,
    out_sem, out_send_sem, out_recv_sem,
):
    tok = TILE_FRAMES * TILE_ROWS * cols
    nk, nz = nt // 2, nh // 2
    chips = nk * nh
    width = GROUP_HEADS * HEAD_DIM
    ta, ha = lax.axis_index("ta"), lax.axis_index("ha")
    kk, core = ta // 2, ta % 2
    zz, half = ha // 2, ha % 2
    chip = kk * nh + ha
    others = [(1 - core, half), (core, 1 - half), (1 - core, 1 - half)]

    def mate(where):
        return (2 * kk + where[0], 2 * zz + where[1])

    have_x = (kk > 0, kk < nk - 1)
    have_z = (zz > 0, zz < nz - 1)
    far_x = (kk == nk // 2, kk == nk // 2 - 1)
    half_tok = tok // 2
    part_rows = (pl.ds(0, half_tok), pl.ds(half_tok, half_tok))

    nothing = jnp.zeros((tok, 2 * HEAD_DIM), BF16)
    for side in range(2):

        @pl.when(jnp.logical_not(have_x[side]))
        def _(side=side):
            def clear(h, carry):
                for n in range(4):
                    ext[h, 3 * side, n] = nothing
                for n in range(2):
                    from_x[h, side, n] = nothing
                return carry

            lax.fori_loop(0, GROUP_HEADS, clear, 0)

        @pl.when(jnp.logical_not(have_x[side]) | far_x[side])
        def _(side=side):
            def clear(h, carry):
                for n in range(2):
                    from_cross[h, side, n] = jnp.zeros((half_tok, 2 * HEAD_DIM), BF16)
                return carry

            lax.fori_loop(0, GROUP_HEADS, clear, 0)

        @pl.when(jnp.logical_not(have_z[side]))
        def _(side=side):
            def clear(h, carry):
                for n in range(4):
                    ext[h, n, 3 * side] = nothing
                    from_z[h, side, n] = nothing
                return carry

            lax.fori_loop(0, GROUP_HEADS, clear, 0)

    barrier = pltpu.get_barrier_semaphore()

    def greet(d, carry):
        to = lax.rem(chip + d, chips)
        pl.semaphore_signal(
            barrier, inc=1, device_id=(2 * (to // nh) + core, to % nh), device_id_type=MESH
        )
        return carry

    lax.fori_loop(1, chips, greet, 0)
    for where in ((1 - core, half), (1 - core, 1 - half)):
        pl.semaphore_signal(barrier, inc=1, device_id=mate(where), device_id_type=MESH)

    seq = (q_ref, k_ref, v_ref)
    own_rows = pl.ds(pl.multiple_of(core * tok, tok), tok)

    def head_cols(h, n, of):
        inner = (n % 2) * width + h * HEAD_DIM
        return pl.ds(pl.multiple_of(of * 2 * width + inner, HEAD_DIM), HEAD_DIM)

    def pair_own(h, n):
        return pltpu.make_async_copy(
            seq[n // 2].at[:, head_cols(h, n, core)],
            pair.at[n // 2, own_rows, head_cols(h, n, 0)],
            pair_sem.at[h, n],
        )

    def start_own(h, carry):
        for n in range(6):
            pair_own(h, n).start()
        return carry

    lax.fori_loop(0, GROUP_HEADS, start_own, 0)

    def group_cols(where, n=width):
        return pl.ds(pl.multiple_of((2 * where[0] + where[1]) * width, width), width)

    own_block = 2 * core + half
    pltpu.make_async_copy(
        grad_ref.at[:, group_cols((core, half))], grad_blocks.at[own_block], grad_sem
    ).start()

    pl.semaphore_wait(barrier, chips + 1)

    def pair_copy(h, n):
        return pltpu.make_async_remote_copy(
            src_ref=seq[n // 2].at[:, head_cols(h, n, 1 - core)],
            dst_ref=pair.at[n // 2, own_rows, head_cols(h, n, 0)],
            send_sem=pair_send_sem.at[h, n],
            recv_sem=pair_recv_sem.at[h, n],
            device_id=mate((1 - core, half)),
            device_id_type=MESH,
        )

    def grad_copy(n):
        return pltpu.make_async_remote_copy(
            src_ref=grad_ref.at[:, group_cols(others[n])],
            dst_ref=grad_blocks.at[own_block],
            send_sem=grad_send_sem.at[n],
            recv_sem=grad_recv_sem.at[n],
            device_id=mate(others[n]),
            device_id_type=MESH,
        )

    def start_pair(h, carry):
        for n in range(6):
            pair_copy(h, n).start()
        return carry

    lax.fori_loop(0, GROUP_HEADS, start_pair, 0)
    for n in range(3):
        grad_copy(n).start()

    def decode(t):
        frame = t // (nh * TILE_ROWS * cols)
        row = (t // cols) % (nh * TILE_ROWS)
        frame_block, row_block = frame // TILE_FRAMES, row // TILE_ROWS
        inside = ((frame % TILE_FRAMES) * TILE_ROWS + row % TILE_ROWS) * cols + t % cols
        return frame_block, row_block, inside

    pieces = tok // order_ref.shape[1]

    def source_rows(first, count, step):
        return jnp.concatenate(
            [order_ref[pl.ds(first * pieces + n, count, step), :] for n in range(pieces)], axis=1
        )

    order = source_rows(0, nt * nh, pieces)
    order_t = order.T
    for cc in range(2):
        source = kk * 2 * nh + cc * nh + ha
        line = source_rows(source, 1, 1)
        column = jnp.sum(
            jnp.where(iota(order_t.shape, 1) == source, order_t, 0), axis=1, keepdims=True
        )
        line_f, line_r, _ = decode(line)
        col_f, col_r, _ = decode(column)
        same = (line_f * nh + line_r) == (col_f * nh + col_r)
        earlier = iota((tok, tok), 0) < iota((tok, tok), 1)
        second = jnp.sum(jnp.where(same & earlier, 1, 0), axis=0, keepdims=True)
        region = (line_f // 2) * nz + line_r // 2
        seat = region * 16 + ((line_f % 2) * 2 + line_r % 2) * 4 + cc * 2 + second
        sort_one[:, cc * tok : (cc + 1) * tok] = jnp.where(
            iota((2 * tok, tok), 0) == seat, 1.0, 0.0
        ).astype(BF16)

    def all_copy(h, d):
        to = lax.rem(chip + d, chips)
        to_k, to_h = to // nh, to % nh
        region = to_k * nz + to_h // 2
        return pltpu.make_async_remote_copy(
            src_ref=send.at[h, to_h % 2, pl.ds(pl.multiple_of(region * 16, 16), 16)],
            dst_ref=recv.at[h, pl.ds(pl.multiple_of(chip * 16, 16), 16)],
            send_sem=all_send_sem.at[h],
            recv_sem=all_recv_sem.at[h],
            device_id=(2 * to_k + core, to_h),
            device_id_type=MESH,
        )

    def all_own(h):
        region = kk * nz + zz
        return pltpu.make_async_copy(
            send.at[h, half, pl.ds(pl.multiple_of(region * 16, 16), 16)],
            recv.at[h, pl.ds(pl.multiple_of(chip * 16, 16), 16)],
            all_sem.at[h],
        )

    def send_head(h, carry):
        for n in range(6):
            pair_own(h, n).wait()
            pair_copy(h, n).wait_recv()
        for a in range(3):
            left = pl.ds(pl.multiple_of(h * HEAD_DIM, HEAD_DIM), HEAD_DIM)
            right = pl.ds(pl.multiple_of(width + h * HEAD_DIM, HEAD_DIM), HEAD_DIM)
            both = jnp.concatenate([pair[a, :, left], pair[a, :, right]], axis=1)
            sorted_rows = dot(sort_one[...], both).astype(BF16)
            into = slice(a * HEAD_DIM, (a + 1) * HEAD_DIM)
            send[h, 0, :, into] = sorted_rows[:, :HEAD_DIM]
            send[h, 1, :, into] = sorted_rows[:, HEAD_DIM:]
        all_own(h).start()

        def push(d, inner):
            all_copy(h, d).start()
            return inner

        lax.fori_loop(1, chips, push, 0)
        return carry

    lax.fori_loop(0, GROUP_HEADS, send_head, 0)

    frame_block, row_block, inside = decode(order_t)
    block_of = frame_block * nh + row_block
    code = iota(order_t.shape, 0) * tok + inside
    found = []
    for b in range(4):
        mine = block_of == (2 * kk + b // 2) * nh + 2 * zz + b % 2
        found.append(jnp.min(jnp.where(mine, code, tok * tok), axis=0, keepdims=True) % tok)
        found.append(jnp.max(jnp.where(mine, code, 0), axis=0, keepdims=True) % tok)
    table = jnp.concatenate(found, axis=0).astype(F32).astype(BF16)
    rows = 4 * tok
    number = iota((nt * nh, rows), 1)
    from_chip, place_in = number // 16, number % 16
    sender = (from_chip // nh) * 2 * nh + ((place_in // 2) % 2) * nh + from_chip % nh
    spread = jnp.where(iota((nt * nh, rows), 0) == sender, 1.0, 0.0).astype(BF16)
    wide = dot(table, spread)
    lane = iota((8, rows), 1) % 16
    chosen = iota((8, rows), 0) == (lane // 4) * 2 + lane % 2
    position = jnp.sum(jnp.where(chosen, wide, 0.0), axis=0, keepdims=True).astype(jnp.int32)
    position = position + (iota((1, rows), 1) % 16 // 4) * tok

    def fill_place(b, carry):
        place[b] = jnp.where(iota((tok, rows), 0) + b * tok == position, 1.0, 0.0).astype(BF16)
        return carry

    lax.fori_loop(0, 4, fill_place, 0)

    pltpu.make_async_copy(
        grad_ref.at[:, group_cols((core, half))], grad_blocks.at[own_block], grad_sem
    ).wait()
    for n in range(3):
        grad_copy(n).wait_recv()

    def turn_grad(b, carry):
        for h in range(GROUP_HEADS):
            piece = grad_blocks[b, :, h * HEAD_DIM : (h + 1) * HEAD_DIM]
            grad_t[h, b] = piece.astype(F32).T.astype(BF16)
        return carry

    lax.fori_loop(0, 4, turn_grad, 0)

    def x_device(side):
        return (ta + 2 * (2 * side - 1), ha)

    def z_device(side):
        return (ta, ha + 2 * (2 * side - 1))

    def remote(src, dst, sends, recvs, index, device):
        return pltpu.make_async_remote_copy(
            src_ref=src, dst_ref=dst, send_sem=sends.at[index], recv_sem=recvs.at[index],
            device_id=device, device_id_type=MESH,
        )

    def x_side(h, side):
        return remote(
            ext.at[h, 1 + side, pl.ds(1, 2)], ext.at[h, 3 - 3 * side, pl.ds(1, 2)],
            side_send_sem, side_recv_sem, (h, side), x_device(side),
        )

    def z_side(h, side):
        return remote(
            ext.at[h, pl.ds(1, 2), 1 + side], ext.at[h, pl.ds(1, 2), 3 - 3 * side],
            side_send_sem, side_recv_sem, (h, 2 + side), z_device(side),
        )

    def corner(h, column, side, part):
        return remote(
            ext.at[h, 3 * column, 1 + side, part_rows[part]],
            ext.at[h, 3 * column, 3 - 3 * side, part_rows[part]],
            corner_send_sem, corner_recv_sem, (h, 4 * part + 2 * column + side), z_device(side),
        )

    def cross(h, column, side):
        return pltpu.make_async_remote_copy(
            src_ref=ext.at[h, 1 + column, 3 * side, part_rows[1]],
            dst_ref=ext.at[h, 3 - 3 * column, 3 * side, part_rows[1]],
            send_sem=cross_send_sem.at[h, 2 * column + side],
            recv_sem=corner_recv_sem.at[h, 4 + 2 * (1 - column) + 1 - side],
            device_id=x_device(column),
            device_id_type=MESH,
        )

    def z_back(h, side, kind, part):
        two = pl.ds(2 * kind, 2)
        return remote(
            back_z.at[h, side, two, part_rows[part]], from_z.at[h, 1 - side, two, part_rows[part]],
            back_z_send_sem, back_z_recv_sem, (h, 2 * (kind + part) + side), z_device(side),
        )

    def z_back_far(h, column, side):
        return remote(
            back_z.at[h, side, column, part_rows[1]], from_z.at[h, 1 - side, column, part_rows[1]],
            back_z_send_sem, back_z_recv_sem, (h, 6 + 2 * column + side), z_device(side),
        )

    def x_back(h, side, part):
        both = pl.ds(0, 2)
        return remote(
            back_x.at[h, side, both, part_rows[part]], from_x.at[h, 1 - side, both, part_rows[part]],
            back_x_send_sem, back_x_recv_sem, (h, 2 * part + side), x_device(side),
        )

    def x_cross(h, column, side):
        return remote(
            back_cross.at[h, column, side], from_cross.at[h, 1 - column, side],
            back_cross_send_sem, back_cross_recv_sem, (h, 2 * column + side), x_device(column),
        )

    def along(have, step):
        for side in range(2):
            pl.when(have[side])(functools.partial(step, side))

    def corners(have, step, only=None):
        for column in range(2):
            for side in range(2):
                when = have_x[column] & have[side]
                if only is not None:
                    when = when & only[column]
                pl.when(when)(functools.partial(step, column, side))

    near_x = tuple(jnp.logical_not(f) for f in far_x)
    came_x, came_z = have_x[::-1], have_z[::-1]
    at_near = tuple(have_x[n] & near_x[n] for n in range(2))
    at_far = tuple(have_x[n] & far_x[n] for n in range(2))

    def gather_in(h, carry):
        all_own(h).wait()
        many = pl.ds(0, 16 * (chips - 1))
        pltpu.make_async_copy(recv.at[h, many], recv.at[h, many], all_recv_sem.at[h]).wait()
        return carry

    lax.fori_loop(0, GROUP_HEADS, gather_in, 0)

    def start_sides(h):
        along(have_x, lambda side: x_side(h, side).start())
        along(have_z, lambda side: z_side(h, side).start())

    def settle(h, carry):
        def one_block(b, inner):
            grid_rows = dot(place[b], recv[h])
            query_t[h, b] = grid_rows[:, :HEAD_DIM].T.astype(BF16)
            ext[h, 1 + b // 2, 1 + b % 2] = grid_rows[:, HEAD_DIM:].astype(BF16)
            return inner

        lax.fori_loop(0, 4, one_block, 0)
        pl.when(h == 0)(lambda: start_sides(0))
        return carry

    lax.fori_loop(0, GROUP_HEADS, settle, 0)

    def pass_corners(h):
        along(came_x, lambda side: x_side(h, side).wait_recv())
        corners(have_z, lambda column, side: corner(h, column, side, 0).start())
        corners(have_z, lambda column, side: corner(h, column, side, 1).start(), far_x)
        along(came_z, lambda side: z_side(h, side).wait_recv())
        corners(have_z, lambda column, side: cross(h, column, side).start(), near_x)

    pass_corners(0)
    start_sides(1)
    start_sides(2)

    def out_cols(h):
        first = ((2 * core + half) * GROUP_HEADS + h) * HEAD_DIM
        return pl.ds(pl.multiple_of(first, HEAD_DIM), HEAD_DIM)

    def out_copy(pair_of, h, n):
        two = pl.ds(2 * pair_of, 2)
        return remote(
            stage.at[h, 2 * others[n][0] + others[n][1], two], out_ref.at[two, :, out_cols(h)],
            out_send_sem, out_recv_sem, pair_of, mate(others[n]),
        )

    def out_own(pair_of, h):
        two = pl.ds(2 * pair_of, 2)
        return pltpu.make_async_copy(
            stage.at[h, own_block, two], out_ref.at[two, :, out_cols(h)], out_sem.at[pair_of]
        )

    def hand_out(pair_of, h):
        for n in (1, 2, 0):
            out_copy(pair_of, h, n).start()
        out_own(pair_of, h).start()

    def bias_of(i, j):
        gone = [jnp.logical_not(have_x[i // 3])] if i in (0, 3) else []
        gone += [jnp.logical_not(have_z[j // 3])] if j in (0, 3) else []
        if not gone:
            return None
        return jnp.where(functools.reduce(jnp.logical_or, gone), NEG, 0.0).astype(F32)

    bias = {(i, j): bias_of(i, j) for i in range(4) for j in range(4)}

    def turn(h):
        first, later = slice(0, half_tok), slice(half_tok, tok)
        along(came_z, lambda side: z_back(h, side, 0, 0).wait_recv())
        for column in range(2):
            for j in range(2):
                both = keep[h, 3 * column, j, first] + from_z[h, j, column, first].astype(F32)
                back_x[h, column, j, first] = both.astype(BF16)
        along(have_x, lambda side: x_back(h, side, 0).start())
        corners(came_z, lambda column, side: z_back_far(h, column, side).wait_recv(), far_x)

        def add_far(column):
            for j in range(2):
                both = keep[h, 3 * column, j, later] + from_z[h, j, column, later].astype(F32)
                back_x[h, column, j, later] = both.astype(BF16)
            x_back(h, column, 1).start()

        along(at_far, add_far)
        for column in range(2):
            for side in range(2):
                pl.when(at_near[1 - column] & have_z[side])(
                    functools.partial(lambda c, d: x_cross(h, c, d).wait_recv(), column, side)
                )
        for side in range(2):
            for i in range(2):
                both = keep_z[h, side, i] + from_cross[h, i, side].astype(F32)
                back_z[h, side, 2 + i, later] = both.astype(BF16)
        along(have_z, lambda side: z_back(h, side, 1, 1).start())

    def finish(h):
        for part in range(2):
            along(came_z, lambda side: z_back(h, side, 1, part).wait_recv())
            along(came_x, lambda side: x_back(h, side, part).wait_recv())
        for b in range(4):
            i, j = b // 2, b % 2
            whole = keep[h, 1 + i, j] + from_z[h, j, 2 + i].astype(F32)
            low = (whole + from_x[h, i, j].astype(F32)).astype(BF16)
            stage[h, b, 2] = low[:, :HEAD_DIM]
            stage[h, b, 3] = low[:, HEAD_DIM:]
        hand_out(1, h)

    def attend(h, carry):
        for part in range(2):
            corners(came_z, lambda column, side: corner(h, column, side, part).wait_recv())

        def prepare(e, inner):
            ext_t[e // 4, e % 4] = ext[h, e // 4, e % 4].astype(F32).T.astype(BF16)
            return inner

        lax.fori_loop(0, 16, prepare, 0)
        top, total, out_t, dq_t = [None] * 4, [None] * 4, [None] * 4, [None] * 4
        delta, inverse = [None] * 4, [None] * 4

        def add(held, b, n, term):
            held[b] = term if n == 0 else held[b] + term

        def scores_of(b, n):
            spot = spots_of(b)[n]
            s = dot(ext[h, spot[0], spot[1], :, :HEAD_DIM], query_t[h, b])
            score[b % 2, n] = s
            most = jnp.max(s, axis=0, keepdims=True)
            if bias[spot] is not None:
                most = most + bias[spot]
            top[b] = most if n == 0 else jnp.maximum(top[b], most)

        def forward(b, n):
            i, j = spots_of(b)[n]
            shift = top[b] * (SCALE * LOG2E)
            if bias[i, j] is not None:
                shift = shift - bias[i, j]
            p = jnp.exp2(score[b % 2, n] * (SCALE * LOG2E) - shift)
            add(total, b, n, jnp.sum(p, axis=0, keepdims=True))
            p_low = p.astype(BF16)
            prob[b, n] = p_low
            add(out_t, b, n, dot(ext_t[i, j, HEAD_DIM:, :], p_low))
            if n == 8:
                inverse[b] = 1.0 / total[b]
                full = out_t[b] * inverse[b]
                grad_f = grad_t[h, b].astype(F32)
                delta[b] = jnp.sum(grad_f * full, axis=0, keepdims=True)
                stage[h, b, 0] = full.T.astype(BF16)
                grad_s[b] = (grad_f * inverse[b]).astype(BF16)
                query_s[b] = (query_t[h, b].astype(F32) * (inverse[b] * SCALE)).astype(BF16)

        def backward(b, n):
            i, j = spots_of(b)[n]
            dp = dot(ext[h, i, j, :, HEAD_DIM:], grad_t[h, b])
            ds = (prob[b, n].astype(F32) * (dp - delta[b])).astype(BF16)
            grad_score[b, n] = ds
            add(dq_t, b, n, dot(ext_t[i, j, :HEAD_DIM, :], ds))
            if n == 8:
                stage[h, b, 1] = (dq_t[b] * (inverse[b] * SCALE)).T.astype(BF16)

        for beat in range(6):
            for n in range(9):
                for step, b in ((scores_of, beat), (forward, beat - 1), (backward, beat - 2)):
                    if 0 <= b < 4:
                        step(b, n)

        hand_out(0, h)

        pl.when(h == 0)(lambda: pass_corners(1))
        pl.when(h > 0)(lambda: turn(h - 1))

        def key_terms(i, j):
            k_sum = v_sum = None
            for b in range(4):
                if (i, j) in spots_of(b):
                    n = spots_of(b).index((i, j))
                    k_term = dot_nt(grad_score[b, n], query_s[b])
                    v_term = dot_nt(prob[b, n], grad_s[b])
                    k_sum = k_term if k_sum is None else k_sum + k_term
                    v_sum = v_term if v_sum is None else v_sum + v_term
            return ((slice(0, HEAD_DIM), k_sum), (slice(HEAD_DIM, 2 * HEAD_DIM), v_sum))

        first, later = slice(0, half_tok), slice(half_tok, tok)
        for side in range(2):
            for column in range(2):
                for lanes, value in key_terms(3 * column, 3 * side):
                    low = value.astype(BF16)
                    back_z[h, side, column, :, lanes] = low
                    back_cross[h, column, side, :, lanes] = low[later]
        along(have_z, lambda side: z_back(h, side, 0, 0).start())
        corners(have_z, lambda column, side: z_back_far(h, column, side).start(), far_x)
        corners(have_z, lambda column, side: x_cross(h, column, side).start(), near_x)
        for column in range(2):
            for j in (1, 2):
                for lanes, value in key_terms(3 * column, j):
                    keep[h, 3 * column, j - 1, :, lanes] = value
                    back_x[h, column, j - 1, later, lanes] = value[later].astype(BF16)
        along(at_near, lambda side: x_back(h, side, 1).start())
        for side in range(2):
            for i in (1, 2):
                for lanes, value in key_terms(i, 3 * side):
                    back_z[h, side, SEAT[i], first, lanes] = value[first].astype(BF16)
                    keep_z[h, side, i - 1, :, lanes] = value[later]
        along(have_z, lambda side: z_back(h, side, 1, 0).start())
        for i in (1, 2):
            for j in (1, 2):
                for lanes, value in key_terms(i, j):
                    keep[h, i, j - 1, :, lanes] = value
        pl.when(h == 0)(lambda: pass_corners(2))
        pl.when(h > 0)(lambda: finish(h - 1))
        return carry

    lax.fori_loop(0, GROUP_HEADS, attend, 0)
    turn(GROUP_HEADS - 1)
    finish(GROUP_HEADS - 1)

    for n in range(3):
        grad_copy(n).wait_send()

    def sent(h, carry):
        for n in range(6):
            pair_copy(h, n).wait_send()
        many = pl.ds(0, 16 * (chips - 1))
        pltpu.make_async_copy(recv.at[h, many], recv.at[h, many], all_send_sem.at[h]).wait()
        along(have_x, lambda side: x_side(h, side).wait_send())
        along(have_z, lambda side: z_side(h, side).wait_send())
        corners(have_z, lambda column, side: corner(h, column, side, 0).wait_send())
        corners(have_z, lambda column, side: corner(h, column, side, 1).wait_send(), far_x)
        corners(have_z, lambda column, side: cross(h, column, side).wait_send(), near_x)
        for kind, part in ((0, 0), (1, 0), (1, 1)):
            along(have_z, lambda side: z_back(h, side, kind, part).wait_send())
        corners(have_z, lambda column, side: z_back_far(h, column, side).wait_send(), far_x)
        corners(have_z, lambda column, side: x_cross(h, column, side).wait_send(), near_x)
        for part in range(2):
            along(have_x, lambda side: x_back(h, side, part).wait_send())
        return carry

    lax.fori_loop(0, GROUP_HEADS, sent, 0)
    for pair_of in range(2):
        two = pl.ds(2 * pair_of, 2)
        mine = out_ref.at[two, :, pl.ds(0, width)]
        far = out_ref.at[two, :, pl.ds(0, 3 * width)]
        pltpu.make_async_copy(mine, mine, out_sem.at[pair_of]).wait()
        pltpu.make_async_copy(far, far, out_send_sem.at[pair_of]).wait()
        pltpu.make_async_copy(far, far, out_recv_sem.at[pair_of]).wait()


def deal(in_ref, *refs):
    outs, (held, in_sem, out_sem) = refs[:4], refs[4:]
    into = [pltpu.make_async_copy(in_ref.at[n], held.at[n], in_sem.at[n]) for n in range(4)]
    onward = [pltpu.make_async_copy(held.at[n], outs[n], out_sem.at[n]) for n in range(4)]
    for copy in into:
        copy.start()
    for n in range(4):
        into[n].wait()
        onward[n].start()
    for copy in onward:
        copy.wait()


def shards(nt, nh, query_seq, key_seq, value_seq, tile_order, grad_output):
    block_shape = grad_output.shape
    cols = block_shape[2]
    tok, channels = query_seq.shape
    low = jax.ShapeDtypeStruct((tok, channels), BF16)
    hbm = pl.BlockSpec(memory_space=pl.ANY)
    vmem = pl.BlockSpec(memory_space=pltpu.VMEM)
    gh, d = GROUP_HEADS, HEAD_DIM
    dma = pltpu.SemaphoreType.DMA
    whole = pl.pallas_call(
        functools.partial(kernel, nt, nh, cols),
        out_shape=jax.ShapeDtypeStruct((4, tok, channels), BF16),
        in_specs=[hbm, hbm, hbm, vmem, hbm],
        out_specs=hbm,
        scratch_shapes=[
            pltpu.VMEM((3, 2 * tok, 2 * gh * d), BF16),
            pltpu.VMEM((2 * tok, 2 * tok), BF16),
            pltpu.VMEM((gh, 2, 2 * tok, 3 * d), BF16),
            pltpu.VMEM((gh, 4 * tok, 3 * d), BF16),
            pltpu.VMEM((4, tok, 4 * tok), BF16),
            pltpu.VMEM((gh, 4, 4, tok, 2 * d), BF16),
            pltpu.VMEM((4, 4, 2 * d, tok), BF16),
            pltpu.VMEM((gh, 4, d, tok), BF16),
            pltpu.VMEM((4, tok, gh * d), BF16),
            pltpu.VMEM((gh, 4, d, tok), BF16),
            pltpu.VMEM((2, 9, tok, tok), F32),
            pltpu.VMEM((4, 9, tok, tok), BF16),
            pltpu.VMEM((4, 9, tok, tok), BF16),
            pltpu.VMEM((4, d, tok), BF16),
            pltpu.VMEM((4, d, tok), BF16),
            pltpu.VMEM((gh, 4, 2, tok, 2 * d), F32),
            pltpu.VMEM((gh, 2, 2, tok // 2, 2 * d), F32),
            pltpu.VMEM((gh, 2, 4, tok, 2 * d), BF16),
            pltpu.VMEM((gh, 2, 4, tok, 2 * d), BF16),
            pltpu.VMEM((gh, 2, 2, tok, 2 * d), BF16),
            pltpu.VMEM((gh, 2, 2, tok, 2 * d), BF16),
            pltpu.VMEM((gh, 2, 2, tok // 2, 2 * d), BF16),
            pltpu.VMEM((gh, 2, 2, tok // 2, 2 * d), BF16),
            pltpu.VMEM((gh, 4, 4, tok, d), BF16),
            dma((gh, 6)), dma((gh, 6)), dma((gh, 6)),
            dma, dma((3,)), dma((3,)),
            dma((gh,)), dma((gh,)), dma((gh,)),
            dma((gh, 4)), dma((gh, 4)), dma((gh, 8)), dma((gh, 8)), dma((gh, 4)),
            dma((gh, 10)), dma((gh, 10)), dma((gh, 4)), dma((gh, 4)), dma((gh, 4)), dma((gh, 4)),
            dma((2,)), dma((2,)), dma((2,)),
        ],
        compiler_params=pltpu.CompilerParams(
            collective_id=0, has_side_effects=True, vmem_limit_bytes=60 * 2**20
        ),
        cost_estimate=pl.CostEstimate(
            flops=12 * 4 * gh * 9 * tok * tok * d,
            bytes_accessed=16 * tok * channels,
            transcendentals=4 * gh * 9 * tok * tok,
        ),
    )(query_seq, key_seq, value_seq, tile_order.reshape(-1, min(tok, 128)), grad_output.reshape(tok, channels))
    outs = pl.pallas_call(
        deal,
        out_shape=[low] * 4,
        in_specs=[hbm],
        out_specs=[hbm] * 4,
        scratch_shapes=[pltpu.VMEM((4, tok, channels), BF16), dma((4,)), dma((4,))],
        compiler_params=pltpu.CompilerParams(vmem_limit_bytes=60 * 2**20),
    )(whole)
    return tuple(o.reshape(block_shape) for o in outs)


def solution(mesh):
    seq = P(("ta", "ha"), None)
    grid = P("ta", "ha", None, None)
    return jax.shard_map(
        functools.partial(shards, mesh.shape["ta"], mesh.shape["ha"]),
        mesh=mesh,
        in_specs=(seq, seq, seq, P(), grid),
        out_specs=(grid,) * 4,
        check_vma=False,
    )
```

```python
import functools

import jax
import jax.numpy as jnp
from jax import lax
from jax.experimental import pallas as pl
from jax.experimental.pallas import tpu as pltpu
from jax.sharding import PartitionSpec as P

HEADS = 12
HEAD_DIM = 128
GROUP_HEADS = 3
TILE_FRAMES = 4
TILE_ROWS = 8
SCALE = HEAD_DIM ** (-0.5)
LOG2E = 1.4426950408889634
NEG = -1e30
MESH = pl.DeviceIdType.MESH
F32 = jnp.float32
BF16 = jnp.bfloat16
SEAT = {0: 0, 3: 1, 1: 2, 2: 3}


def dot(a, b):
    return jnp.dot(a, b, preferred_element_type=F32)


def dot_nt(a, b):
    return lax.dot_general(a, b, (((1,), (1,)), ((), ())), preferred_element_type=F32)


def iota(shape, dim):
    return lax.broadcasted_iota(jnp.int32, shape, dim)


def spots_of(b):
    return [(b // 2 + di, b % 2 + dj) for di in range(3) for dj in range(3)]


def kernel(
    nt, nh, cols,
    q_ref, k_ref, v_ref, order_ref, grad_ref,
    out_ref,
    pair, sort_one, send, recv, place, ext, ext_t, query_t, grad_blocks, grad_t,
    score, prob, grad_score, query_s, grad_s, keep, keep_z,
    back_z, from_z, back_x, from_x, back_cross, from_cross, stage,
    pair_sem, pair_send_sem, pair_recv_sem,
    grad_sem, grad_send_sem, grad_recv_sem,
    all_sem, all_send_sem, all_recv_sem,
    side_send_sem, side_recv_sem, corner_send_sem, corner_recv_sem, cross_send_sem,
    back_z_send_sem, back_z_recv_sem, back_x_send_sem, back_x_recv_sem,
    back_cross_send_sem, back_cross_recv_sem,
    out_sem, out_send_sem, out_recv_sem,
):
    tok = TILE_FRAMES * TILE_ROWS * cols
    nk, nz = nt // 2, nh // 2
    chips = nk * nh
    width = GROUP_HEADS * HEAD_DIM
    ta, ha = lax.axis_index("ta"), lax.axis_index("ha")
    kk, core = ta // 2, ta % 2
    zz, half = ha // 2, ha % 2
    chip = kk * nh + ha
    others = [(1 - core, half), (core, 1 - half), (1 - core, 1 - half)]

    def mate(where):
        return (2 * kk + where[0], 2 * zz + where[1])

    have_x = (kk > 0, kk < nk - 1)
    have_z = (zz > 0, zz < nz - 1)
    far_x = (kk == nk // 2, kk == nk // 2 - 1)
    half_tok = tok // 2
    part_rows = (pl.ds(0, half_tok), pl.ds(half_tok, half_tok))

    nothing = jnp.zeros((tok, 2 * HEAD_DIM), BF16)
    for side in range(2):

        @pl.when(jnp.logical_not(have_x[side]))
        def _(side=side):
            def clear(h, carry):
                for n in range(4):
                    ext[h, 3 * side, n] = nothing
                for n in range(2):
                    from_x[h, side, n] = nothing
                return carry

            lax.fori_loop(0, GROUP_HEADS, clear, 0)

        @pl.when(jnp.logical_not(have_x[side]) | far_x[side])
        def _(side=side):
            def clear(h, carry):
                for n in range(2):
                    from_cross[h, side, n] = jnp.zeros((half_tok, 2 * HEAD_DIM), BF16)
                return carry

            lax.fori_loop(0, GROUP_HEADS, clear, 0)

        @pl.when(jnp.logical_not(have_z[side]))
        def _(side=side):
            def clear(h, carry):
                for n in range(4):
                    ext[h, n, 3 * side] = nothing
                    from_z[h, side, n] = nothing
                return carry

            lax.fori_loop(0, GROUP_HEADS, clear, 0)

    barrier = pltpu.get_barrier_semaphore()

    def greet(d, carry):
        to = lax.rem(chip + d, chips)
        pl.semaphore_signal(
            barrier, inc=1, device_id=(2 * (to // nh) + core, to % nh), device_id_type=MESH
        )
        return carry

    lax.fori_loop(1, chips, greet, 0)
    for where in ((1 - core, half), (1 - core, 1 - half)):
        pl.semaphore_signal(barrier, inc=1, device_id=mate(where), device_id_type=MESH)

    seq = (q_ref, k_ref, v_ref)
    own_rows = pl.ds(pl.multiple_of(core * tok, tok), tok)

    def head_cols(h, n, of):
        inner = (n % 2) * width + h * HEAD_DIM
        return pl.ds(pl.multiple_of(of * 2 * width + inner, HEAD_DIM), HEAD_DIM)

    def pair_own(h, n):
        return pltpu.make_async_copy(
            seq[n // 2].at[:, head_cols(h, n, core)],
            pair.at[n // 2, own_rows, head_cols(h, n, 0)],
            pair_sem.at[h, n],
        )

    def start_own(h, carry):
        for n in range(6):
            pair_own(h, n).start()
        return carry

    lax.fori_loop(0, GROUP_HEADS, start_own, 0)

    def group_cols(where, n=width):
        return pl.ds(pl.multiple_of((2 * where[0] + where[1]) * width, width), width)

    own_block = 2 * core + half
    pltpu.make_async_copy(
        grad_ref.at[:, group_cols((core, half))], grad_blocks.at[own_block], grad_sem
    ).start()

    pl.semaphore_wait(barrier, chips + 1)

    def pair_copy(h, n):
        return pltpu.make_async_remote_copy(
            src_ref=seq[n // 2].at[:, head_cols(h, n, 1 - core)],
            dst_ref=pair.at[n // 2, own_rows, head_cols(h, n, 0)],
            send_sem=pair_send_sem.at[h, n],
            recv_sem=pair_recv_sem.at[h, n],
            device_id=mate((1 - core, half)),
            device_id_type=MESH,
        )

    def grad_copy(n):
        return pltpu.make_async_remote_copy(
            src_ref=grad_ref.at[:, group_cols(others[n])],
            dst_ref=grad_blocks.at[own_block],
            send_sem=grad_send_sem.at[n],
            recv_sem=grad_recv_sem.at[n],
            device_id=mate(others[n]),
            device_id_type=MESH,
        )

    def start_pair(h, carry):
        for n in range(6):
            pair_copy(h, n).start()
        return carry

    lax.fori_loop(0, GROUP_HEADS, start_pair, 0)
    for n in range(3):
        grad_copy(n).start()

    def decode(t):
        frame = t // (nh * TILE_ROWS * cols)
        row = (t // cols) % (nh * TILE_ROWS)
        frame_block, row_block = frame // TILE_FRAMES, row // TILE_ROWS
        inside = ((frame % TILE_FRAMES) * TILE_ROWS + row % TILE_ROWS) * cols + t % cols
        return frame_block, row_block, inside

    pieces = tok // order_ref.shape[1]

    def source_rows(first, count, step):
        return jnp.concatenate(
            [order_ref[pl.ds(first * pieces + n, count, step), :] for n in range(pieces)], axis=1
        )

    order = source_rows(0, nt * nh, pieces)
    order_t = order.T
    for cc in range(2):
        source = kk * 2 * nh + cc * nh + ha
        line = source_rows(source, 1, 1)
        column = jnp.sum(
            jnp.where(iota(order_t.shape, 1) == source, order_t, 0), axis=1, keepdims=True
        )
        line_f, line_r, _ = decode(line)
        col_f, col_r, _ = decode(column)
        same = (line_f * nh + line_r) == (col_f * nh + col_r)
        earlier = iota((tok, tok), 0) < iota((tok, tok), 1)
        second = jnp.sum(jnp.where(same & earlier, 1, 0), axis=0, keepdims=True)
        region = (line_f // 2) * nz + line_r // 2
        seat = region * 16 + ((line_f % 2) * 2 + line_r % 2) * 4 + cc * 2 + second
        sort_one[:, cc * tok : (cc + 1) * tok] = jnp.where(
            iota((2 * tok, tok), 0) == seat, 1.0, 0.0
        ).astype(BF16)

    def all_copy(h, d):
        to = lax.rem(chip + d, chips)
        to_k, to_h = to // nh, to % nh
        region = to_k * nz + to_h // 2
        return pltpu.make_async_remote_copy(
            src_ref=send.at[h, to_h % 2, pl.ds(pl.multiple_of(region * 16, 16), 16)],
            dst_ref=recv.at[h, pl.ds(pl.multiple_of(chip * 16, 16), 16)],
            send_sem=all_send_sem.at[h],
            recv_sem=all_recv_sem.at[h],
            device_id=(2 * to_k + core, to_h),
            device_id_type=MESH,
        )

    def all_own(h):
        region = kk * nz + zz
        return pltpu.make_async_copy(
            send.at[h, half, pl.ds(pl.multiple_of(region * 16, 16), 16)],
            recv.at[h, pl.ds(pl.multiple_of(chip * 16, 16), 16)],
            all_sem.at[h],
        )

    def send_head(h, carry):
        for n in range(6):
            pair_own(h, n).wait()
            pair_copy(h, n).wait_recv()
        for a in range(3):
            left = pl.ds(pl.multiple_of(h * HEAD_DIM, HEAD_DIM), HEAD_DIM)
            right = pl.ds(pl.multiple_of(width + h * HEAD_DIM, HEAD_DIM), HEAD_DIM)
            both = jnp.concatenate([pair[a, :, left], pair[a, :, right]], axis=1)
            sorted_rows = dot(sort_one[...], both).astype(BF16)
            into = slice(a * HEAD_DIM, (a + 1) * HEAD_DIM)
            send[h, 0, :, into] = sorted_rows[:, :HEAD_DIM]
            send[h, 1, :, into] = sorted_rows[:, HEAD_DIM:]
        all_own(h).start()

        def push(d, inner):
            all_copy(h, d).start()
            return inner

        lax.fori_loop(1, chips, push, 0)
        return carry

    lax.fori_loop(0, GROUP_HEADS, send_head, 0)

    frame_block, row_block, inside = decode(order_t)
    block_of = frame_block * nh + row_block
    code = iota(order_t.shape, 0) * tok + inside
    found = []
    for b in range(4):
        mine = block_of == (2 * kk + b // 2) * nh + 2 * zz + b % 2
        found.append(jnp.min(jnp.where(mine, code, tok * tok), axis=0, keepdims=True) % tok)
        found.append(jnp.max(jnp.where(mine, code, 0), axis=0, keepdims=True) % tok)
    table = jnp.concatenate(found, axis=0).astype(F32).astype(BF16)
    rows = 4 * tok
    number = iota((nt * nh, rows), 1)
    from_chip, place_in = number // 16, number % 16
    sender = (from_chip // nh) * 2 * nh + ((place_in // 2) % 2) * nh + from_chip % nh
    spread = jnp.where(iota((nt * nh, rows), 0) == sender, 1.0, 0.0).astype(BF16)
    wide = dot(table, spread)
    lane = iota((8, rows), 1) % 16
    chosen = iota((8, rows), 0) == (lane // 4) * 2 + lane % 2
    position = jnp.sum(jnp.where(chosen, wide, 0.0), axis=0, keepdims=True).astype(jnp.int32)
    position = position + (iota((1, rows), 1) % 16 // 4) * tok

    def fill_place(b, carry):
        place[b] = jnp.where(iota((tok, rows), 0) + b * tok == position, 1.0, 0.0).astype(BF16)
        return carry

    lax.fori_loop(0, 4, fill_place, 0)

    pltpu.make_async_copy(
        grad_ref.at[:, group_cols((core, half))], grad_blocks.at[own_block], grad_sem
    ).wait()
    for n in range(3):
        grad_copy(n).wait_recv()

    def turn_grad(b, carry):
        for h in range(GROUP_HEADS):
            piece = grad_blocks[b, :, h * HEAD_DIM : (h + 1) * HEAD_DIM]
            grad_t[h, b] = piece.astype(F32).T.astype(BF16)
        return carry

    lax.fori_loop(0, 4, turn_grad, 0)

    def x_device(side):
        return (ta + 2 * (2 * side - 1), ha)

    def z_device(side):
        return (ta, ha + 2 * (2 * side - 1))

    def remote(src, dst, sends, recvs, index, device):
        return pltpu.make_async_remote_copy(
            src_ref=src, dst_ref=dst, send_sem=sends.at[index], recv_sem=recvs.at[index],
            device_id=device, device_id_type=MESH,
        )

    def x_side(h, side):
        return remote(
            ext.at[h, 1 + side, pl.ds(1, 2)], ext.at[h, 3 - 3 * side, pl.ds(1, 2)],
            side_send_sem, side_recv_sem, (h, side), x_device(side),
        )

    def z_side(h, side):
        return remote(
            ext.at[h, pl.ds(1, 2), 1 + side], ext.at[h, pl.ds(1, 2), 3 - 3 * side],
            side_send_sem, side_recv_sem, (h, 2 + side), z_device(side),
        )

    def corner(h, column, side, part):
        return remote(
            ext.at[h, 3 * column, 1 + side, part_rows[part]],
            ext.at[h, 3 * column, 3 - 3 * side, part_rows[part]],
            corner_send_sem, corner_recv_sem, (h, 4 * part + 2 * column + side), z_device(side),
        )

    def cross(h, column, side):
        return pltpu.make_async_remote_copy(
            src_ref=ext.at[h, 1 + column, 3 * side, part_rows[1]],
            dst_ref=ext.at[h, 3 - 3 * column, 3 * side, part_rows[1]],
            send_sem=cross_send_sem.at[h, 2 * column + side],
            recv_sem=corner_recv_sem.at[h, 4 + 2 * (1 - column) + 1 - side],
            device_id=x_device(column),
            device_id_type=MESH,
        )

    def z_back(h, side, kind, part):
        two = pl.ds(2 * kind, 2)
        return remote(
            back_z.at[h, side, two, part_rows[part]], from_z.at[h, 1 - side, two, part_rows[part]],
            back_z_send_sem, back_z_recv_sem, (h, 2 * (kind + part) + side), z_device(side),
        )

    def z_back_far(h, column, side):
        return remote(
            back_z.at[h, side, column, part_rows[1]], from_z.at[h, 1 - side, column, part_rows[1]],
            back_z_send_sem, back_z_recv_sem, (h, 6 + 2 * column + side), z_device(side),
        )

    def x_back(h, side, part):
        both = pl.ds(0, 2)
        return remote(
            back_x.at[h, side, both, part_rows[part]], from_x.at[h, 1 - side, both, part_rows[part]],
            back_x_send_sem, back_x_recv_sem, (h, 2 * part + side), x_device(side),
        )

    def x_cross(h, column, side):
        return remote(
            back_cross.at[h, column, side], from_cross.at[h, 1 - column, side],
            back_cross_send_sem, back_cross_recv_sem, (h, 2 * column + side), x_device(column),
        )

    def along(have, step):
        for side in range(2):
            pl.when(have[side])(functools.partial(step, side))

    def corners(have, step, only=None):
        for column in range(2):
            for side in range(2):
                when = have_x[column] & have[side]
                if only is not None:
                    when = when & only[column]
                pl.when(when)(functools.partial(step, column, side))

    near_x = tuple(jnp.logical_not(f) for f in far_x)
    came_x, came_z = have_x[::-1], have_z[::-1]
    at_near = tuple(have_x[n] & near_x[n] for n in range(2))
    at_far = tuple(have_x[n] & far_x[n] for n in range(2))

    def gather_in(h, carry):
        all_own(h).wait()
        many = pl.ds(0, 16 * (chips - 1))
        pltpu.make_async_copy(recv.at[h, many], recv.at[h, many], all_recv_sem.at[h]).wait()
        return carry

    lax.fori_loop(0, GROUP_HEADS, gather_in, 0)

    def start_sides(h):
        along(have_x, lambda side: x_side(h, side).start())
        along(have_z, lambda side: z_side(h, side).start())

    def settle(h, carry):
        def one_block(b, inner):
            grid_rows = dot(place[b], recv[h])
            query_t[h, b] = grid_rows[:, :HEAD_DIM].T.astype(BF16)
            ext[h, 1 + b // 2, 1 + b % 2] = grid_rows[:, HEAD_DIM:].astype(BF16)
            return inner

        lax.fori_loop(0, 4, one_block, 0)
        pl.when(h == 0)(lambda: start_sides(0))
        return carry

    lax.fori_loop(0, GROUP_HEADS, settle, 0)

    def pass_corners(h):
        along(came_x, lambda side: x_side(h, side).wait_recv())
        corners(have_z, lambda column, side: corner(h, column, side, 0).start())
        corners(have_z, lambda column, side: corner(h, column, side, 1).start(), far_x)
        along(came_z, lambda side: z_side(h, side).wait_recv())
        corners(have_z, lambda column, side: cross(h, column, side).start(), near_x)

    pass_corners(0)
    start_sides(1)
    start_sides(2)

    def out_cols(h):
        first = ((2 * core + half) * GROUP_HEADS + h) * HEAD_DIM
        return pl.ds(pl.multiple_of(first, HEAD_DIM), HEAD_DIM)

    def out_copy(pair_of, h, n):
        two = pl.ds(2 * pair_of, 2)
        return remote(
            stage.at[h, 2 * others[n][0] + others[n][1], two], out_ref.at[two, :, out_cols(h)],
            out_send_sem, out_recv_sem, pair_of, mate(others[n]),
        )

    def out_own(pair_of, h):
        two = pl.ds(2 * pair_of, 2)
        return pltpu.make_async_copy(
            stage.at[h, own_block, two], out_ref.at[two, :, out_cols(h)], out_sem.at[pair_of]
        )

    def hand_out(pair_of, h):
        for n in (1, 2, 0):
            out_copy(pair_of, h, n).start()
        out_own(pair_of, h).start()

    def bias_of(i, j):
        gone = [jnp.logical_not(have_x[i // 3])] if i in (0, 3) else []
        gone += [jnp.logical_not(have_z[j // 3])] if j in (0, 3) else []
        if not gone:
            return None
        return jnp.where(functools.reduce(jnp.logical_or, gone), NEG, 0.0).astype(F32)

    bias = {(i, j): bias_of(i, j) for i in range(4) for j in range(4)}

    def turn(h):
        first, later = slice(0, half_tok), slice(half_tok, tok)
        along(came_z, lambda side: z_back(h, side, 0, 0).wait_recv())
        for column in range(2):
            for j in range(2):
                both = keep[h, 3 * column, j, first] + from_z[h, j, column, first].astype(F32)
                back_x[h, column, j, first] = both.astype(BF16)
        along(have_x, lambda side: x_back(h, side, 0).start())
        corners(came_z, lambda column, side: z_back_far(h, column, side).wait_recv(), far_x)

        def add_far(column):
            for j in range(2):
                both = keep[h, 3 * column, j, later] + from_z[h, j, column, later].astype(F32)
                back_x[h, column, j, later] = both.astype(BF16)
            x_back(h, column, 1).start()

        along(at_far, add_far)
        for column in range(2):
            for side in range(2):
                pl.when(at_near[1 - column] & have_z[side])(
                    functools.partial(lambda c, d: x_cross(h, c, d).wait_recv(), column, side)
                )
        for side in range(2):
            for i in range(2):
                both = keep_z[h, side, i] + from_cross[h, i, side].astype(F32)
                back_z[h, side, 2 + i, later] = both.astype(BF16)
        along(have_z, lambda side: z_back(h, side, 1, 1).start())

    def finish(h):
        for part in range(2):
            along(came_z, lambda side: z_back(h, side, 1, part).wait_recv())
            along(came_x, lambda side: x_back(h, side, part).wait_recv())
        for n in (1, 2, 0, None):
            i, j = (core, half) if n is None else others[n]
            b = 2 * i + j
            whole = keep[h, 1 + i, j] + from_z[h, j, 2 + i].astype(F32)
            low = (whole + from_x[h, i, j].astype(F32)).astype(BF16)
            stage[h, b, 2] = low[:, :HEAD_DIM]
            stage[h, b, 3] = low[:, HEAD_DIM:]
            if n is None:
                out_own(1, h).start()
            else:
                out_copy(1, h, n).start()

    def attend(h, carry):
        for part in range(2):
            corners(came_z, lambda column, side: corner(h, column, side, part).wait_recv())

        def prepare(e, inner):
            ext_t[e // 4, e % 4] = ext[h, e // 4, e % 4].astype(F32).T.astype(BF16)
            return inner

        lax.fori_loop(0, 16, prepare, 0)
        top, total, out_t, dq_t = [None] * 4, [None] * 4, [None] * 4, [None] * 4
        delta, inverse = [None] * 4, [None] * 4

        def add(held, b, n, term):
            held[b] = term if n == 0 else held[b] + term

        def scores_of(b, n):
            spot = spots_of(b)[n]
            s = dot(ext[h, spot[0], spot[1], :, :HEAD_DIM], query_t[h, b])
            score[b % 2, n] = s
            most = jnp.max(s, axis=0, keepdims=True)
            if bias[spot] is not None:
                most = most + bias[spot]
            top[b] = most if n == 0 else jnp.maximum(top[b], most)

        def forward(b, n):
            i, j = spots_of(b)[n]
            shift = top[b] * (SCALE * LOG2E)
            if bias[i, j] is not None:
                shift = shift - bias[i, j]
            p = jnp.exp2(score[b % 2, n] * (SCALE * LOG2E) - shift)
            add(total, b, n, jnp.sum(p, axis=0, keepdims=True))
            p_low = p.astype(BF16)
            prob[b, n] = p_low
            add(out_t, b, n, dot(ext_t[i, j, HEAD_DIM:, :], p_low))
            if n == 8:
                inverse[b] = 1.0 / total[b]
                full = out_t[b] * inverse[b]
                grad_f = grad_t[h, b].astype(F32)
                delta[b] = jnp.sum(grad_f * full, axis=0, keepdims=True)
                stage[h, b, 0] = full.T.astype(BF16)
                grad_s[b] = (grad_f * inverse[b]).astype(BF16)
                query_s[b] = (query_t[h, b].astype(F32) * (inverse[b] * SCALE)).astype(BF16)

        def backward(b, n):
            i, j = spots_of(b)[n]
            dp = dot(ext[h, i, j, :, HEAD_DIM:], grad_t[h, b])
            ds = (prob[b, n].astype(F32) * (dp - delta[b])).astype(BF16)
            grad_score[b, n] = ds
            add(dq_t, b, n, dot(ext_t[i, j, :HEAD_DIM, :], ds))
            if n == 8:
                stage[h, b, 1] = (dq_t[b] * (inverse[b] * SCALE)).T.astype(BF16)

        for beat in range(6):
            for n in range(9):
                for step, b in ((scores_of, beat), (forward, beat - 1), (backward, beat - 2)):
                    if 0 <= b < 4:
                        step(b, n)

        hand_out(0, h)

        pl.when(h == 0)(lambda: pass_corners(1))
        pl.when(h > 0)(lambda: turn(h - 1))

        def key_terms(i, j):
            k_sum = v_sum = None
            for b in range(4):
                if (i, j) in spots_of(b):
                    n = spots_of(b).index((i, j))
                    k_term = dot_nt(grad_score[b, n], query_s[b])
                    v_term = dot_nt(prob[b, n], grad_s[b])
                    k_sum = k_term if k_sum is None else k_sum + k_term
                    v_sum = v_term if v_sum is None else v_sum + v_term
            return ((slice(0, HEAD_DIM), k_sum), (slice(HEAD_DIM, 2 * HEAD_DIM), v_sum))

        first, later = slice(0, half_tok), slice(half_tok, tok)
        for side in range(2):
            for column in range(2):
                for lanes, value in key_terms(3 * column, 3 * side):
                    low = value.astype(BF16)
                    back_z[h, side, column, :, lanes] = low
                    back_cross[h, column, side, :, lanes] = low[later]
        along(have_z, lambda side: z_back(h, side, 0, 0).start())
        corners(have_z, lambda column, side: z_back_far(h, column, side).start(), far_x)
        corners(have_z, lambda column, side: x_cross(h, column, side).start(), near_x)
        for column in range(2):
            for j in (1, 2):
                for lanes, value in key_terms(3 * column, j):
                    keep[h, 3 * column, j - 1, :, lanes] = value
                    back_x[h, column, j - 1, later, lanes] = value[later].astype(BF16)
        along(at_near, lambda side: x_back(h, side, 1).start())
        for side in range(2):
            for i in (1, 2):
                for lanes, value in key_terms(i, 3 * side):
                    back_z[h, side, SEAT[i], first, lanes] = value[first].astype(BF16)
                    keep_z[h, side, i - 1, :, lanes] = value[later]
        along(have_z, lambda side: z_back(h, side, 1, 0).start())
        for i in (1, 2):
            for j in (1, 2):
                for lanes, value in key_terms(i, j):
                    keep[h, i, j - 1, :, lanes] = value
        pl.when(h == 0)(lambda: pass_corners(2))
        pl.when(h > 0)(lambda: finish(h - 1))
        return carry

    lax.fori_loop(0, GROUP_HEADS, attend, 0)
    turn(GROUP_HEADS - 1)
    finish(GROUP_HEADS - 1)

    for n in range(3):
        grad_copy(n).wait_send()

    def sent(h, carry):
        for n in range(6):
            pair_copy(h, n).wait_send()
        many = pl.ds(0, 16 * (chips - 1))
        pltpu.make_async_copy(recv.at[h, many], recv.at[h, many], all_send_sem.at[h]).wait()
        along(have_x, lambda side: x_side(h, side).wait_send())
        along(have_z, lambda side: z_side(h, side).wait_send())
        corners(have_z, lambda column, side: corner(h, column, side, 0).wait_send())
        corners(have_z, lambda column, side: corner(h, column, side, 1).wait_send(), far_x)
        corners(have_z, lambda column, side: cross(h, column, side).wait_send(), near_x)
        for kind, part in ((0, 0), (1, 0), (1, 1)):
            along(have_z, lambda side: z_back(h, side, kind, part).wait_send())
        corners(have_z, lambda column, side: z_back_far(h, column, side).wait_send(), far_x)
        corners(have_z, lambda column, side: x_cross(h, column, side).wait_send(), near_x)
        for part in range(2):
            along(have_x, lambda side: x_back(h, side, part).wait_send())
        return carry

    lax.fori_loop(0, GROUP_HEADS, sent, 0)
    for pair_of in range(2):
        two = pl.ds(2 * pair_of, 2)
        mine = out_ref.at[two, :, pl.ds(0, width)]
        far = out_ref.at[two, :, pl.ds(0, 3 * width)]
        pltpu.make_async_copy(mine, mine, out_sem.at[pair_of]).wait()
        pltpu.make_async_copy(far, far, out_send_sem.at[pair_of]).wait()
        pltpu.make_async_copy(far, far, out_recv_sem.at[pair_of]).wait()


def deal(in_ref, *refs):
    outs, (held, in_sem, out_sem) = refs[:4], refs[4:]
    into = [pltpu.make_async_copy(in_ref.at[n], held.at[n], in_sem.at[n]) for n in range(4)]
    onward = [pltpu.make_async_copy(held.at[n], outs[n], out_sem.at[n]) for n in range(4)]
    for copy in into:
        copy.start()
    for n in range(4):
        into[n].wait()
        onward[n].start()
    for copy in onward:
        copy.wait()


def shards(nt, nh, query_seq, key_seq, value_seq, tile_order, grad_output):
    block_shape = grad_output.shape
    cols = block_shape[2]
    tok, channels = query_seq.shape
    low = jax.ShapeDtypeStruct((tok, channels), BF16)
    hbm = pl.BlockSpec(memory_space=pl.ANY)
    vmem = pl.BlockSpec(memory_space=pltpu.VMEM)
    gh, d = GROUP_HEADS, HEAD_DIM
    dma = pltpu.SemaphoreType.DMA
    whole = pl.pallas_call(
        functools.partial(kernel, nt, nh, cols),
        out_shape=jax.ShapeDtypeStruct((4, tok, channels), BF16),
        in_specs=[hbm, hbm, hbm, vmem, hbm],
        out_specs=hbm,
        scratch_shapes=[
            pltpu.VMEM((3, 2 * tok, 2 * gh * d), BF16),
            pltpu.VMEM((2 * tok, 2 * tok), BF16),
            pltpu.VMEM((gh, 2, 2 * tok, 3 * d), BF16),
            pltpu.VMEM((gh, 4 * tok, 3 * d), BF16),
            pltpu.VMEM((4, tok, 4 * tok), BF16),
            pltpu.VMEM((gh, 4, 4, tok, 2 * d), BF16),
            pltpu.VMEM((4, 4, 2 * d, tok), BF16),
            pltpu.VMEM((gh, 4, d, tok), BF16),
            pltpu.VMEM((4, tok, gh * d), BF16),
            pltpu.VMEM((gh, 4, d, tok), BF16),
            pltpu.VMEM((2, 9, tok, tok), F32),
            pltpu.VMEM((4, 9, tok, tok), BF16),
            pltpu.VMEM((4, 9, tok, tok), BF16),
            pltpu.VMEM((4, d, tok), BF16),
            pltpu.VMEM((4, d, tok), BF16),
            pltpu.VMEM((gh, 4, 2, tok, 2 * d), F32),
            pltpu.VMEM((gh, 2, 2, tok // 2, 2 * d), F32),
            pltpu.VMEM((gh, 2, 4, tok, 2 * d), BF16),
            pltpu.VMEM((gh, 2, 4, tok, 2 * d), BF16),
            pltpu.VMEM((gh, 2, 2, tok, 2 * d), BF16),
            pltpu.VMEM((gh, 2, 2, tok, 2 * d), BF16),
            pltpu.VMEM((gh, 2, 2, tok // 2, 2 * d), BF16),
            pltpu.VMEM((gh, 2, 2, tok // 2, 2 * d), BF16),
            pltpu.VMEM((gh, 4, 4, tok, d), BF16),
            dma((gh, 6)), dma((gh, 6)), dma((gh, 6)),
            dma, dma((3,)), dma((3,)),
            dma((gh,)), dma((gh,)), dma((gh,)),
            dma((gh, 4)), dma((gh, 4)), dma((gh, 8)), dma((gh, 8)), dma((gh, 4)),
            dma((gh, 10)), dma((gh, 10)), dma((gh, 4)), dma((gh, 4)), dma((gh, 4)), dma((gh, 4)),
            dma((2,)), dma((2,)), dma((2,)),
        ],
        compiler_params=pltpu.CompilerParams(
            collective_id=0, has_side_effects=True, vmem_limit_bytes=60 * 2**20
        ),
        cost_estimate=pl.CostEstimate(
            flops=12 * 4 * gh * 9 * tok * tok * d,
            bytes_accessed=16 * tok * channels,
            transcendentals=4 * gh * 9 * tok * tok,
        ),
    )(query_seq, key_seq, value_seq, tile_order.reshape(-1, min(tok, 128)), grad_output.reshape(tok, channels))
    outs = pl.pallas_call(
        deal,
        out_shape=[low] * 4,
        in_specs=[hbm],
        out_specs=[hbm] * 4,
        scratch_shapes=[pltpu.VMEM((4, tok, channels), BF16), dma((4,)), dma((4,))],
        compiler_params=pltpu.CompilerParams(vmem_limit_bytes=60 * 2**20),
    )(whole)
    return tuple(o.reshape(block_shape) for o in outs)


def solution(mesh):
    seq = P(("ta", "ha"), None)
    grid = P("ta", "ha", None, None)
    return jax.shard_map(
        functools.partial(shards, mesh.shape["ta"], mesh.shape["ha"]),
        mesh=mesh,
        in_specs=(seq, seq, seq, P(), grid),
        out_specs=(grid,) * 4,
        check_vma=False,
    )
```
